32 devices in a mesh: stack: 2 (over x), lat: 16 (over z, y, core).
Axes of the slice: x: 2, y: 2, z: 4, core: 2. Of those that a mesh axis runs over, the one named last changes fastest.
Arguments:
- solution: float32 [8, 1024, 1024], P('stack', 'lat'), parts along dimension 0, may hold values from -10 to 10
- residual: float32 [8, 1024, 1024], P('stack', 'lat'), parts along dimension 0, may hold values from -10 to 10
- gradient: float32 [8, 1024, 1024], P('stack', 'lat'), parts along dimension 0, may hold values from -10 to 10
- direction: float32 [8, 1024, 1024], P('stack', 'lat'), parts along dimension 0, may hold values from -10 to 10
- row_taps: float32 [4, 4, 31], replicated, may hold values from -0.5 to 0.5
- col_taps: float32 [4, 4, 31], replicated, may hold values from -1 to 1
- damping: float32 [1], replicated, may hold values from 0.3 to 3
Outputs:
- new_solution: float32 [8, 1024, 1024], P('stack', 'lat'), parts along dimension 0
- new_residual: float32 [8, 1024, 1024], P('stack', 'lat'), parts along dimension 0
- new_gradient: float32 [8, 1024, 1024], P('stack', 'lat'), parts along dimension 0
- new_direction: float32 [8, 1024, 1024], P('stack', 'lat'), parts along dimension 0
The draws below stay inside these ranges and needn't reach their ends.
There are 2 independent parts, one for each index of `stack`. The reference program is written for one: setup_inputs(seed, part) draws one part's arguments, and reference() takes and returns one part's arrays. A program takes and returns all parts, laid end to end along the dimension named above; an argument that names none is the same for every part. Nothing has to cross between parts.
All inputs are finite; a program needn't handle non-finite values.
Results may differ from the reference program's by a relative error of at most 0.000094.
Values sent between devices are 32-bit elements; how exact they have to be, the bound alone decides.
No kernel may reach another device: no remote copies, remote signals or barrier semaphores. Data moves between devices by JAX's collectives and lax.ppermute only.
A program may use at most 64 MiB of HBM per device.

```python
import math
import jax
import jax.numpy as jnp
from jax import lax

PLANES = 4
COLS = 1024
TAPS = 31
ROWS = 1024


def rough_field(key, noise_scale):
    key_noise = jax.random.fold_in(key, 0)
    row_ramp = 1.0 + jnp.arange(ROWS, dtype=jnp.float32)[None, :, None] / max(ROWS - 1, 1)
    values = noise_scale * jax.random.normal(key_noise, (PLANES, ROWS, COLS), jnp.float32) * row_ramp
    return values


def wave_field(key, waves, period):
    key_rowfreq, key_colfreq, key_phase, key_amp = jax.random.split(key, 4)
    row_freq = jax.random.randint(key_rowfreq, (PLANES, waves), 1, 25).astype(jnp.int32)
    col_freq = jax.random.randint(key_colfreq, (PLANES, waves), -24, 25).astype(jnp.int32)
    phases = jax.random.randint(key_phase, (PLANES, waves), 0, period).astype(jnp.int32)
    amplitudes = jax.random.uniform(key_amp, (PLANES, waves), jnp.float32, 0.35, 0.75)
    row_index = jnp.arange(ROWS, dtype=jnp.int32)[None, :, None]
    col_index = jnp.arange(COLS, dtype=jnp.int32)[None, None, :]
    total = jnp.zeros((PLANES, ROWS, COLS), jnp.float32)
    for wave in range(waves):
        turns = (row_index * row_freq[:, wave][:, None, None] + col_index * col_freq[:, wave][:, None, None] + phases[:, wave][:, None, None]) % period
        angle = turns.astype(jnp.float32) * (2.0 * math.pi / period)
        total = total + amplitudes[:, wave][:, None, None] * jnp.cos(angle)
    return total


def field_draw(key, offset_seed):
    noise_key = jax.random.fold_in(key, offset_seed)
    return jnp.clip(rough_field(noise_key, 1.0), -10.0, 10.0)


def draw_solution(key, part):
    return field_draw(key, 11)


def draw_residual(key, part):
    return field_draw(key, 23)


def draw_gradient(key, part):
    return field_draw(key, 37)


def draw_direction(key, part):
    key = jax.random.fold_in(key, 41)
    key_rough, key_waves = jax.random.split(key, 2)
    values = rough_field(key_rough, 0.7) + wave_field(key_waves, 6, 256)
    return jnp.clip(values, -10.0, 10.0)


def bell_draw(own_key, shape, width, bound, kind=jnp.bfloat16):
    entries = jax.random.normal(own_key, shape, jnp.float32) * width
    return jnp.minimum(jnp.maximum(entries, -bound), bound).astype(kind)


def setup_inputs(seed: int = 0, part: int = 0) -> dict:
    streams_of = jax.random.split(jax.random.key(seed), 8)
    part_splits = jax.random.split(jax.random.fold_in(streams_of[7], part), 8)
    return {
        "solution": draw_solution(jax.random.fold_in(jax.random.fold_in(streams_of[7], part), 71), part),
        "residual": draw_residual(jax.random.fold_in(jax.random.fold_in(streams_of[7], part), 71), part),
        "gradient": draw_gradient(jax.random.fold_in(jax.random.fold_in(streams_of[7], part), 71), part),
        "direction": draw_direction(jax.random.fold_in(jax.random.fold_in(streams_of[7], part), 71), part),
        "row_taps": bell_draw(streams_of[4], (PLANES, PLANES, TAPS), (TAPS * PLANES) ** -0.5, 0.5, jnp.float32),
        "col_taps": bell_draw(streams_of[5], (PLANES, PLANES, TAPS), TAPS ** -0.5, 1.0, jnp.float32),
        "damping": jnp.clip(jnp.exp(jax.random.uniform(streams_of[6], (1,), jnp.float32, math.log(0.3), math.log(3.0))), 0.3, 3.0),
    }


def operate(padded, row_kernel, col_kernel):
    depth = padded.shape[0]
    taps_count = row_kernel.shape[2]
    border = taps_count // 2
    out_rows = padded.shape[1] - (taps_count - 1)
    columns = padded.shape[2]

    def one_source(source, running):
        source_plane = lax.dynamic_index_in_dim(padded, source, 0, keepdims=False)
        widened = jnp.pad(source_plane, ((0, 0), (border, border)))
        row_now = lax.dynamic_index_in_dim(row_kernel, source, 1, keepdims=False)
        col_now = lax.dynamic_index_in_dim(col_kernel, source, 1, keepdims=False)
        along_cols = jnp.zeros((depth, source_plane.shape[0], columns), jnp.float32)
        for offset in range(taps_count):
            along_cols = along_cols + col_now[:, offset][:, None, None] * widened[None, :, offset:offset + columns]
        for offset in range(taps_count):
            running = running + row_now[:, offset][:, None, None] * along_cols[:, offset:offset + out_rows, :]
        return running

    initial = jnp.zeros((depth, out_rows, columns), jnp.float32)
    return lax.fori_loop(0, depth, one_source, initial)


def pad_rows(field, border):
    return jnp.pad(field, ((0, 0), (border, border), (0, 0)))


def reference(solution, residual, gradient, direction, row_taps, col_taps, damping):
    border = TAPS // 2
    row_adjoint = jnp.transpose(row_taps, (1, 0, 2))[:, :, ::-1]
    col_adjoint = jnp.transpose(col_taps, (1, 0, 2))[:, :, ::-1]
    damping_value = damping[0]
    norm_before = jnp.sum(gradient * gradient)
    forward_image = operate(pad_rows(direction, border), row_taps, col_taps)
    curvature = jnp.sum(forward_image * forward_image) + damping_value * jnp.sum(direction * direction)
    step_size = norm_before / curvature
    new_solution = solution + step_size * direction
    new_residual = residual - step_size * forward_image
    new_gradient = operate(pad_rows(new_residual, border), row_adjoint, col_adjoint) - damping_value * new_solution
    norm_after = jnp.sum(new_gradient * new_gradient)
    new_direction = new_gradient + (norm_after / norm_before) * direction
    return new_solution, new_residual, new_gradient, new_direction
```

```python
import functools

import jax
import jax.numpy as jnp
from jax import lax
from jax.experimental import pallas as pl
from jax.experimental.pallas import tpu as pltpu
from jax.sharding import PartitionSpec as P

F32 = jnp.float32
BF16 = jnp.bfloat16
EDGE = 16
LANE = 128
PAD = 128
VM = pl.BlockSpec(memory_space=pltpu.VMEM)
SM = pl.BlockSpec(memory_space=pltpu.SMEM)
LIMIT = 40 * 2**20


def split(x):
    hi = x.astype(BF16)
    return hi, (x - hi.astype(F32)).astype(BF16)


def params():
    return pltpu.CompilerParams(vmem_limit_bytes=LIMIT)


def cost(flops, moved):
    return pl.CostEstimate(flops=int(flops), bytes_accessed=int(moved), transcendentals=0)


def row_base(taps, gap):
    hi = lax.reduce_precision(taps, 8, 7)
    lo = taps - hi
    place = lambda t, at: jnp.pad(t, ((0, 0), (0, 0), (at, 256 - at - t.shape[2])))
    return place(hi, 0) + place(hi, gap) + place(lo, 2 * gap)


def col_base(taps):
    hi = lax.reduce_precision(taps, 8, 7)
    lo = taps - hi
    count = taps.shape[2]

    def place(t):
        wide = jnp.pad(t[:, :, ::-1], ((0, 0), (0, 0), (0, 256 - count)))
        return jnp.roll(wide, 1 - count, axis=2)

    return place(hi), jnp.roll(place(lo), LANE, axis=2)


def prep_kernel(depth, inner, taps_e, taps_l, col_hi, col_lo, r_early, r_late, c_out):
    window = 160
    lane = lax.broadcasted_iota(jnp.int32, (window, 256), 1)
    for o in range(depth):
        for s in range(depth):
            base = jnp.broadcast_to(taps_e[o, pl.ds(s, 1), :], (inner, 256))
            rolled = pltpu.roll(base, 1, 1, stride=1, stride_axis=0)
            r_early[s, o * inner:(o + 1) * inner, :] = rolled.astype(BF16)
            base = jnp.broadcast_to(taps_l[o, pl.ds(s, 1), :], (EDGE, 256))
            rolled = pltpu.roll(base, 1, 1, stride=1, stride_axis=0)
            r_late[s, o * EDGE:(o + 1) * EDGE, :] = rolled.astype(BF16)
            hi = jnp.broadcast_to(col_hi[o, pl.ds(s, 1), :], (window, 256))
            lo = jnp.broadcast_to(col_lo[o, pl.ds(s, 1), :], (window, 256))
            hi = pltpu.roll(hi, 0, 1, stride=1, stride_axis=0)
            lo = pltpu.roll(lo, 0, 1, stride=1, stride_axis=0)
            c_out[o, s * 256:s * 256 + window, :] = jnp.where(lane < LANE, hi, lo).astype(BF16)
            c_out[o, s * 256 + window:(s + 1) * 256, :] = jnp.zeros((256 - window, 256), BF16)


def prep(row, col, inner):
    depth = row.shape[0]
    hi, lo = col_base(col)
    return pl.pallas_call(
        functools.partial(prep_kernel, depth, inner),
        out_shape=(
            jax.ShapeDtypeStruct((depth, depth * inner, 256), BF16),
            jax.ShapeDtypeStruct((depth, depth * EDGE, 256), BF16),
            jax.ShapeDtypeStruct((depth, depth * 256, 256), BF16),
        ),
        in_specs=[VM] * 4,
        out_specs=[VM] * 3,
        compiler_params=params(),
        name="prep",
    )(row_base(row, inner + 2 * EDGE), row_base(row, 3 * EDGE), hi, lo)


def shifted(x, border):
    wide = jnp.concatenate([x, jnp.zeros((x.shape[0], PAD), F32)], axis=1)
    return split(pltpu.roll(wide, border, 1))


def put(win, at, group, hi, lo):
    rows = hi.shape[0]
    for g, part in enumerate((hi, lo, hi)):
        win[pl.ds(pl.multiple_of(at + g * group, EDGE), rows), :] = part


def along_columns(v_hi, v_lo, c_ref, o, rows, columns, depth):
    tall = []
    for part in (v_hi, v_lo):
        for n in range(columns // LANE):
            tall.append(jnp.concatenate(
                [part[s, o * rows:(o + 1) * rows, n * LANE:n * LANE + 256] for s in range(depth)], axis=1))
    got = jnp.dot(jnp.concatenate(tall, axis=0), c_ref[o], preferred_element_type=F32)
    blocks = columns // LANE
    out = []
    for n in range(blocks):
        top = got[n * rows:(n + 1) * rows]
        low = got[(blocks + n) * rows:(blocks + n + 1) * rows]
        out.append(top[:, :LANE] + (top[:, LANE:] + low[:, :LANE]))
    return jnp.concatenate(out, axis=1)


def early_kernel(border, odd_ref, v_ref, near_ref, r_ref, c_ref, out_ref, win, v_hi, v_lo):
    depth, rows, columns = v_ref.shape
    inner = rows - EDGE
    group = rows + EDGE
    odd = odd_ref[0]
    for s in range(depth):
        win[s, 3 * group:, :] = jnp.zeros((256 - 3 * group, columns + PAD), BF16)
        put(win.at[s], odd * EDGE, group, *shifted(v_ref[s], border))
        put(win.at[s], (1 - odd) * rows, group, *shifted(near_ref[s], border))
        got = jnp.dot(r_ref[s], win[s], preferred_element_type=F32)
        hi, lo = split(got)
        v_hi[s], v_lo[s] = hi, lo
    for o in range(depth):
        out_ref[o] = along_columns(v_hi, v_lo, c_ref, o, inner, columns, depth)


def early(odd, v, near, r, c, border):
    depth, rows, columns = v.shape
    inner = rows - EDGE
    wide = columns + PAD
    return pl.pallas_call(
        functools.partial(early_kernel, border),
        out_shape=jax.ShapeDtypeStruct((depth, inner, columns), F32),
        in_specs=[SM, VM, VM, VM, VM],
        out_specs=VM,
        scratch_shapes=[
            pltpu.VMEM((depth, 256, wide), BF16),
            pltpu.VMEM((depth, depth * inner, wide), BF16),
            pltpu.VMEM((depth, depth * inner, wide), BF16),
        ],
        compiler_params=params(),
        cost_estimate=cost(2 * depth * depth * 2 * inner * 8 * 256 * 256, 8 * 2**20),
        name="early",
    )(odd, v, near, r, c)


def late_kernel(border, odd_ref, v_ref, far_ref, r_ref, c_ref, out_ref, win, v_hi, v_lo):
    depth, rows, columns = v_ref.shape
    group = 3 * EDGE
    odd = odd_ref[0]
    start = pl.multiple_of(odd * (rows - 2 * EDGE), EDGE)
    for s in range(depth):
        win[s, 3 * group:, :] = jnp.zeros((256 - 3 * group, columns + PAD), BF16)
        put(win.at[s], (1 - odd) * EDGE, group, *shifted(v_ref[s, pl.ds(start, 2 * EDGE), :], border))
        put(win.at[s], odd * 2 * EDGE, group, *shifted(far_ref[s], border))
        got = jnp.dot(r_ref[s], win[s], preferred_element_type=F32)
        hi, lo = split(got)
        v_hi[s], v_lo[s] = hi, lo
    for o in range(depth):
        out_ref[o] = along_columns(v_hi, v_lo, c_ref, o, EDGE, columns, depth)


def late(odd, v, far, r, c, border):
    depth, rows, columns = v.shape
    wide = columns + PAD
    return pl.pallas_call(
        functools.partial(late_kernel, border),
        out_shape=jax.ShapeDtypeStruct((depth, EDGE, columns), F32),
        in_specs=[SM, VM, VM, VM, VM],
        out_specs=VM,
        scratch_shapes=[
            pltpu.VMEM((depth, 256, wide), BF16),
            pltpu.VMEM((depth, depth * EDGE, wide), BF16),
            pltpu.VMEM((depth, depth * EDGE, wide), BF16),
        ],
        compiler_params=params(),
        cost_estimate=cost(2 * depth * depth * 2 * EDGE * 8 * 256 * 256, 4 * 2**20),
        name="late",
    )(odd, v, far, r, c)


def total(axis, values):
    peers = lax.axis_size(axis)
    step = 1
    while step < peers:
        values = values + lax.ppermute(values, axis, [(i, i ^ step) for i in range(peers)])
        step *= 2
    return values


def body(solution, residual, gradient, direction, row_taps, col_taps, damping):
    border = row_taps.shape[2] // 2
    depth, rows, columns = direction.shape
    inner = rows - EDGE
    peers = lax.axis_size("lat")
    odd = lax.axis_index("lat") % 2
    odd_arr = jnp.full((1,), odd, jnp.int32)
    near_pairs = [(i, i ^ 1) for i in range(peers)]
    far_pairs = [p for a in range(1, peers - 1, 2) for p in ((a, a + 1), (a + 1, a))]

    def near_far(v):
        far = lax.dynamic_slice_in_dim(v, odd * inner, EDGE, axis=1)
        near = lax.dynamic_slice_in_dim(v, (1 - odd) * inner, EDGE, axis=1)
        return lax.ppermute(near, "lat", near_pairs), lax.ppermute(far, "lat", far_pairs)

    def whole(a, b):
        return jnp.where(odd == 1, jnp.concatenate([a, b], axis=1), jnp.concatenate([b, a], axis=1))

    row_adjoint = jnp.transpose(row_taps, (1, 0, 2))[:, :, ::-1]
    col_adjoint = jnp.transpose(col_taps, (1, 0, 2))[:, :, ::-1]
    damp = damping[0]

    p_near, p_far = near_far(direction)
    r_near, r_far = near_far(residual)
    re, rl, c = prep(row_taps, col_taps, inner)
    rae, ral, ca = prep(row_adjoint, col_adjoint, inner)

    image_in = early(odd_arr, direction, p_near, re, c, border)
    image_out = late(odd_arr, direction, p_far, rl, c, border)
    image = whole(image_in, image_out)
    f_near, f_far = near_far(image)
    g_in = early(odd_arr, residual, r_near, rae, ca, border)
    g_out = late(odd_arr, residual, r_far, ral, ca, border)
    back_r = whole(g_in, g_out) - damp * solution
    h_in = early(odd_arr, image, f_near, rae, ca, border)
    h_out = late(odd_arr, image, f_far, ral, ca, border)
    back_f = whole(h_in, h_out) + damp * direction

    sums = jnp.stack([
        jnp.sum(gradient * gradient),
        jnp.sum(image * image),
        jnp.sum(direction * direction),
        jnp.sum(back_r * back_r),
        jnp.sum(back_r * back_f),
        jnp.sum(back_f * back_f),
    ])
    sums = total("lat", sums)
    norm_before, image_total, direction_total, rr, rf, ff = (sums[k] for k in range(6))
    curvature = image_total + damp * direction_total
    step = norm_before / curvature
    norm_after = rr - step * (2.0 * rf - step * ff)
    new_solution = solution + step * direction
    new_residual = residual - step * image
    new_gradient = back_r - step * back_f
    new_direction = new_gradient + norm_after / norm_before * direction
    return (new_solution, new_residual, new_gradient, new_direction)


def solution(mesh):
    split_rows = P("stack", "lat", None)
    return jax.shard_map(
        body,
        mesh=mesh,
        in_specs=(split_rows,) * 4 + (P(),) * 3,
        out_specs=(split_rows,) * 4,
        check_vma=False,
    )
```

```python
import functools

import jax
import jax.numpy as jnp
from jax import lax
from jax.experimental import pallas as pl
from jax.experimental.pallas import tpu as pltpu
from jax.sharding import PartitionSpec as P

F32 = jnp.float32
BF16 = jnp.bfloat16
EDGE = 16
LANE = 128
WIDE = 256
VM = pl.BlockSpec(memory_space=pltpu.VMEM)
SM = pl.BlockSpec(memory_space=pltpu.SMEM)
ANY = pl.BlockSpec(memory_space=pl.ANY)
LIMIT = 40 * 2**20


def split(x):
    hi = x.astype(BF16)
    return hi, (x - hi.astype(F32)).astype(BF16)


def params():
    return pltpu.CompilerParams(vmem_limit_bytes=LIMIT)


def cost(us):
    return pl.CostEstimate(flops=int(us * 1.0e9), bytes_accessed=1 << 20, transcendentals=0)


def f32(*shape):
    return jax.ShapeDtypeStruct(shape, F32)


def edges_kernel(odd_ref, p_ref, r_ref, p_far, p_near, r_far, r_near, sems):
    inner = p_ref.shape[1] - EDGE
    odd = odd_ref[0]
    far = pl.multiple_of(odd * inner, EDGE)
    near = pl.multiple_of((1 - odd) * inner, EDGE)
    copies = []
    for k, (src, at, dst) in enumerate(((p_ref, far, p_far), (p_ref, near, p_near), (r_ref, far, r_far), (r_ref, near, r_near))):
        copies.append(pltpu.make_async_copy(src.at[:, pl.ds(at, EDGE), :], dst, sems.at[k]))
    for c in copies:
        c.start()
    for c in copies:
        c.wait()


def edges(odd, p, r):
    depth, rows, columns = p.shape
    return pl.pallas_call(
        edges_kernel,
        out_shape=(f32(depth, EDGE, columns),) * 4,
        in_specs=[SM, ANY, ANY],
        out_specs=[VM] * 4,
        scratch_shapes=[pltpu.SemaphoreType.DMA((4,))],
        compiler_params=params(),
        cost_estimate=cost(1.0),
        name="edges",
    )(odd, p, r)


def one_hot(count, at):
    tap = lax.broadcasted_iota(jnp.int32, (count, WIDE), 0)
    lane = lax.broadcasted_iota(jnp.int32, (count, WIDE), 1)
    return jnp.where(lane == (at(tap) + WIDE) % WIDE, 1.0, 0.0).astype(BF16)


def pick(parts_and_places):
    got = None
    for part, place in parts_and_places:
        term = jnp.dot(part, place, preferred_element_type=F32)
        got = term if got is None else got + term
    return got


def prep_kernel(depth, inner, row_ref, col_ref, *refs):
    outs, bases = refs[:6], refs[6:]
    count = row_ref.shape[1]
    last = count - 1
    row_hi, row_lo = split(row_ref[...])
    col_hi, col_lo = split(col_ref[...])
    window = LANE + 2 * EDGE
    lane = lax.broadcasted_iota(jnp.int32, (window, WIDE), 1)
    for adjoint in (False, True):
        r_early, r_late, c_out = outs[3:] if adjoint else outs[:3]
        turn = (lambda a: last - a) if adjoint else (lambda a: a)
        for base, gap in ((bases[0], inner + 2 * EDGE), (bases[1], 3 * EDGE)):
            base[...] = pick((
                (row_hi, one_hot(count, turn)),
                (row_hi, one_hot(count, lambda a: turn(a) + gap)),
                (row_lo, one_hot(count, lambda a: turn(a) + 2 * gap)),
            ))
        bases[2][...] = pick(((col_hi, one_hot(count, lambda a: -turn(a))),))
        bases[3][...] = pick(((col_lo, one_hot(count, lambda a: LANE - turn(a))),))

        def banded(base, pair, rows, shift):
            wide = jnp.broadcast_to(base[pl.ds(pair, 1), :], (rows, WIDE))
            return pltpu.roll(wide, shift, 1, stride=1, stride_axis=0)

        for o in range(depth):
            for s in range(depth):
                pair = s * depth + o if adjoint else o * depth + s
                r_early[s, o * inner:(o + 1) * inner, :] = banded(bases[0], pair, inner, 1).astype(BF16)
                r_late[s, o * EDGE:(o + 1) * EDGE, :] = banded(bases[1], pair, EDGE, 1).astype(BF16)
                band = jnp.where(lane < LANE, banded(bases[2], pair, window, 0), banded(bases[3], pair, window, 0))
                c_out[o, s * WIDE:s * WIDE + window, :] = band.astype(BF16)
                c_out[o, s * WIDE + window:(s + 1) * WIDE, :] = jnp.zeros((WIDE - window, WIDE), BF16)


def prep(row, col, inner):
    depth, _, count = row.shape
    pairs = depth * depth
    one = (
        jax.ShapeDtypeStruct((depth, depth * inner, WIDE), BF16),
        jax.ShapeDtypeStruct((depth, depth * EDGE, WIDE), BF16),
        jax.ShapeDtypeStruct((depth, depth * WIDE, WIDE), BF16),
    )
    return pl.pallas_call(
        functools.partial(prep_kernel, depth, inner),
        out_shape=one + one,
        in_specs=[VM] * 2,
        out_specs=[VM] * 6,
        scratch_shapes=[pltpu.VMEM((pairs, WIDE), F32)] * 4,
        compiler_params=params(),
        cost_estimate=cost(1.5),
        name="prep",
    )(row.reshape(pairs, count), col.reshape(pairs, count))


def shifted(x, border):
    wide = jnp.concatenate([x, jnp.zeros((x.shape[0], LANE), F32)], axis=1)
    return split(pltpu.roll(wide, border, 1))


def put(win, at, group, hi, lo):
    rows = hi.shape[0]
    for g, part in enumerate((hi, lo, hi)):
        win[pl.ds(pl.multiple_of(at + g * group, EDGE), rows), :] = part


def along_rows(r_ref, win, v_hi, v_lo, s, group):
    if 3 * group < WIDE:
        win[s, 3 * group:, :] = jnp.zeros((WIDE - 3 * group, win.shape[2]), BF16)
    got = jnp.dot(r_ref[s], win[s], preferred_element_type=F32)
    v_hi[s], v_lo[s] = split(got)


def along_columns(v_hi, v_lo, c_ref, o, rows, columns, depth):
    tall = []
    blocks = columns // LANE
    for part in (v_hi, v_lo):
        for n in range(blocks):
            tall.append(jnp.concatenate(
                [part[s, o * rows:(o + 1) * rows, n * LANE:n * LANE + WIDE] for s in range(depth)], axis=1))
    got = jnp.dot(jnp.concatenate(tall, axis=0), c_ref[o], preferred_element_type=F32)
    out = []
    for n in range(blocks):
        top = got[n * rows:(n + 1) * rows]
        low = got[(blocks + n) * rows:(blocks + n + 1) * rows]
        out.append(top[:, :LANE] + (top[:, LANE:] + low[:, :LANE]))
    return jnp.concatenate(out, axis=1)


def folded(x):
    part = jnp.sum(x.reshape(x.shape[0] // 8, 8, x.shape[1]), axis=0)
    part = sum(part[:, n:n + LANE] for n in range(0, x.shape[1], LANE))
    return jnp.sum(part, axis=0, keepdims=True)


def early_kernel(border, odd_ref, v_ref, near_ref, r_ref, c_ref, out_ref, win, v_hi, v_lo):
    depth, rows, columns = v_ref.shape
    inner = rows - EDGE
    group = rows + EDGE
    odd = odd_ref[0]
    for s in range(depth):
        put(win.at[s], odd * EDGE, group, *shifted(v_ref[s], border))
        put(win.at[s], (1 - odd) * rows, group, *shifted(near_ref[s], border))
        along_rows(r_ref, win, v_hi, v_lo, s, group)
    for o in range(depth):
        out_ref[o] = along_columns(v_hi, v_lo, c_ref, o, inner, columns, depth)


def early(odd, v, near, r, c, border):
    depth, rows, columns = v.shape
    inner = rows - EDGE
    wide = columns + LANE
    return pl.pallas_call(
        functools.partial(early_kernel, border),
        out_shape=f32(depth, inner, columns),
        in_specs=[SM, VM, VM, VM, VM],
        out_specs=VM,
        scratch_shapes=[
            pltpu.VMEM((depth, WIDE, wide), BF16),
            pltpu.VMEM((depth, depth * inner, wide), BF16),
            pltpu.VMEM((depth, depth * inner, wide), BF16),
        ],
        compiler_params=params(),
        cost_estimate=cost(2.8),
        name="early",
    )(odd, v, near, r, c)


def late_rows(border, odd, v_ref, far_ref, r_ref, win, v_hi, v_lo):
    depth, rows, _ = v_ref.shape
    group = 3 * EDGE
    start = pl.multiple_of(odd * (rows - 2 * EDGE), EDGE)
    for s in range(depth):
        put(win.at[s], (1 - odd) * EDGE, group, *shifted(v_ref[s, pl.ds(start, 2 * EDGE), :], border))
        put(win.at[s], odd * 2 * EDGE, group, *shifted(far_ref[s], border))
        along_rows(r_ref, win, v_hi, v_lo, s, group)


def late_scratch(depth, columns):
    wide = columns + LANE
    return [
        pltpu.VMEM((depth, WIDE, wide), BF16),
        pltpu.VMEM((depth, depth * EDGE, wide), BF16),
        pltpu.VMEM((depth, depth * EDGE, wide), BF16),
    ]


def image_kernel(border, odd_ref, v_ref, far_ref, r_ref, c_ref, in_ref, grad_ref, out_ref, edge_ref, sums_ref, win, v_hi, v_lo):
    depth, rows, columns = v_ref.shape
    inner = rows - EDGE
    odd = odd_ref[0]
    late_rows(border, odd, v_ref, far_ref, r_ref, win, v_hi, v_lo)
    sums_ref[...] = jnp.zeros_like(sums_ref)
    for o in range(depth):
        edge = along_columns(v_hi, v_lo, c_ref, o, EDGE, columns, depth)
        edge_ref[o] = edge
        out_ref[o, pl.ds(pl.multiple_of(odd * inner, EDGE), EDGE), :] = edge
        out_ref[o, pl.ds(pl.multiple_of((1 - odd) * EDGE, EDGE), inner), :] = in_ref[o]
        sums_ref[0:1, :] += folded(grad_ref[o] * grad_ref[o])
        sums_ref[1:2, :] += folded(in_ref[o] * in_ref[o]) + folded(edge * edge)
        sums_ref[2:3, :] += folded(v_ref[o] * v_ref[o])


def image_late(odd, v, far, r, c, inside, grad, border):
    depth, rows, columns = v.shape
    return pl.pallas_call(
        functools.partial(image_kernel, border),
        out_shape=(f32(depth, rows, columns), f32(depth, EDGE, columns), f32(8, LANE)),
        in_specs=[SM] + [VM] * 6,
        out_specs=[VM] * 3,
        scratch_shapes=late_scratch(depth, columns),
        compiler_params=params(),
        cost_estimate=cost(1.8),
        name="image_late",
    )(odd, v, far, r, c, inside, grad)


def back_kernel(border, odd_ref, damp_ref, v_ref, far_ref, r_ref, c_ref, in_ref, with_ref, out_ref, win, v_hi, v_lo):
    depth, rows, columns = v_ref.shape
    inner = rows - EDGE
    odd = odd_ref[0]
    damp = damp_ref[0]
    late_rows(border, odd, v_ref, far_ref, r_ref, win, v_hi, v_lo)
    for o in range(depth):
        edge = along_columns(v_hi, v_lo, c_ref, o, EDGE, columns, depth)
        at, rest = pl.multiple_of(odd * inner, EDGE), pl.multiple_of((1 - odd) * EDGE, EDGE)
        out_ref[o, pl.ds(at, EDGE), :] = edge - damp * with_ref[o, pl.ds(at, EDGE), :]
        out_ref[o, pl.ds(rest, inner), :] = in_ref[o] - damp * with_ref[o, pl.ds(rest, inner), :]


def back_late(odd, damp, v, far, r, c, inside, beside, border):
    depth, rows, columns = v.shape
    return pl.pallas_call(
        functools.partial(back_kernel, border),
        out_shape=f32(depth, rows, columns),
        in_specs=[SM, SM] + [VM] * 6,
        out_specs=VM,
        scratch_shapes=late_scratch(depth, columns),
        compiler_params=params(),
        cost_estimate=cost(1.6),
        name="back_late",
    )(odd, damp, v, far, r, c, inside, beside)


def last_kernel(border, odd_ref, damp_ref, v_ref, far_ref, r_ref, c_ref, in_ref, with_ref, g_ref, before_ref, out_ref, sums_ref, win, v_hi, v_lo):
    depth, rows, columns = v_ref.shape
    inner = rows - EDGE
    odd = odd_ref[0]
    damp = damp_ref[0]
    late_rows(border, odd, v_ref, far_ref, r_ref, win, v_hi, v_lo)
    sums_ref[...] = before_ref[...]
    for o in range(depth):
        edge = along_columns(v_hi, v_lo, c_ref, o, EDGE, columns, depth)
        for at, rows_now, value in (
            (pl.multiple_of(odd * inner, EDGE), EDGE, edge),
            (pl.multiple_of((1 - odd) * EDGE, EDGE), inner, in_ref[o]),
        ):
            here = pl.ds(at, rows_now)
            h = value + damp * with_ref[o, here, :]
            g = g_ref[o, here, :]
            out_ref[o, here, :] = h
            sums_ref[3:4, :] += folded(g * g)
            sums_ref[4:5, :] += folded(g * h)
            sums_ref[5:6, :] += folded(h * h)


def last_late(odd, damp, v, far, r, c, inside, beside, g, before, border):
    depth, rows, columns = v.shape
    return pl.pallas_call(
        functools.partial(last_kernel, border),
        out_shape=(f32(depth, rows, columns), f32(8, LANE)),
        in_specs=[SM, SM] + [VM] * 8,
        out_specs=[VM] * 2,
        scratch_shapes=late_scratch(depth, columns),
        compiler_params=params(),
        cost_estimate=cost(1.8),
        name="last_late",
    )(odd, damp, v, far, r, c, inside, beside, g, before)


def final_kernel(damp_ref, mine_ref, other_ref, x_ref, r_ref, p_ref, f_ref, g_ref, h_ref,
                 nx_out, nr_out, ng_out, np_out, nx, nr, ng, nd, sems):
    depth = x_ref.shape[0]
    damp = damp_ref[0]
    sums = jnp.sum(mine_ref[...] + other_ref[...], axis=1, keepdims=True)
    before, image, direction, gg, gh, hh = (sums[k:k + 1, :] for k in range(6))
    step = before / (image + damp * direction)
    after = gg - step * (2.0 * gh - step * hh)
    ratio = after / before
    copies = []
    for o in range(depth):
        p = p_ref[o]
        new = g_ref[o] - step * h_ref[o]
        for k, (buf, out, value) in enumerate((
            (nx, nx_out, x_ref[o] + step * p),
            (nr, nr_out, r_ref[o] - step * f_ref[o]),
            (ng, ng_out, new),
            (nd, np_out, new + ratio * p),
        )):
            buf[o] = value
            copies.append(pltpu.make_async_copy(buf.at[o], out.at[o], sems.at[o, k]))
            copies[-1].start()
    for c in copies:
        c.wait()


def final(damp, mine, other, x, r, p, f, g, h):
    shape = x.shape
    return pl.pallas_call(
        final_kernel,
        out_shape=(f32(*shape),) * 4,
        in_specs=[SM] + [VM] * 8,
        out_specs=[ANY] * 4,
        scratch_shapes=[pltpu.VMEM(shape, F32)] * 4 + [pltpu.SemaphoreType.DMA((shape[0], 4))],
        compiler_params=params(),
        cost_estimate=cost(2.0),
        name="final",
    )(damp, mine, other, x, r, p, f, g, h)


def swap(values, axis, step):
    return lax.ppermute(values, axis, [(i, i ^ step) for i in range(lax.axis_size(axis))])


def body(solution, residual, gradient, direction, row_taps, col_taps, damping):
    border = row_taps.shape[2] // 2
    depth, rows, columns = direction.shape
    inner = rows - EDGE
    peers = lax.axis_size("lat")
    odd = lax.axis_index("lat") % 2
    odd_arr = jnp.full((1,), odd, jnp.int32)
    far_pairs = [p for a in range(1, peers - 1, 2) for p in ((a, a + 1), (a + 1, a))]

    def near_swap(v):
        return swap(v, "lat", 1)

    def far_swap(v):
        return lax.ppermute(v, "lat", far_pairs)

    p_far_edge, p_near_edge, r_far_edge, r_near_edge = edges(odd_arr, direction, residual)
    p_far, p_near = far_swap(p_far_edge), near_swap(p_near_edge)
    r_far, r_near = far_swap(r_far_edge), near_swap(r_near_edge)
    re, rl, c, rae, ral, ca = prep(row_taps, col_taps, inner)

    image_in = early(odd_arr, direction, p_near, re, c, border)
    f_near = near_swap(lax.dynamic_slice_in_dim(image_in, (1 - odd) * (inner - EDGE), EDGE, axis=1))
    image, f_edge, sums = image_late(odd_arr, direction, p_far, rl, c, image_in, gradient, border)
    f_far = far_swap(f_edge)
    g_in = early(odd_arr, residual, r_near, rae, ca, border)
    g = back_late(odd_arr, damping, residual, r_far, ral, ca, g_in, solution, border)
    h_in = early(odd_arr, image, f_near, rae, ca, border)
    h, sums = last_late(odd_arr, damping, image, f_far, ral, ca, h_in, direction, g, sums, border)

    step = 1
    while 2 * step < peers:
        sums = sums + swap(sums, "lat", step)
        step *= 2
    other = swap(sums, "lat", step)
    return final(damping, sums, other, solution, residual, direction, image, g, h)


def solution(mesh):
    split_rows = P("stack", "lat", None)
    return jax.shard_map(
        body,
        mesh=mesh,
        in_specs=(split_rows,) * 4 + (P(),) * 3,
        out_specs=(split_rows,) * 4,
        check_vma=False,
    )
```

```python
import functools

import jax
import jax.numpy as jnp
from jax import lax
from jax.experimental import pallas as pl
from jax.experimental.pallas import tpu as pltpu
from jax.sharding import PartitionSpec as P

F32 = jnp.float32
BF16 = jnp.bfloat16
EDGE = 16
LANE = 128
WIDE = 256
VM = pl.BlockSpec(memory_space=pltpu.VMEM)
SM = pl.BlockSpec(memory_space=pltpu.SMEM)
ANY = pl.BlockSpec(memory_space=pl.ANY)
LIMIT = 20 * 2**20


def split(x):
    hi = x.astype(BF16)
    return hi, (x - hi.astype(F32)).astype(BF16)


def params():
    return pltpu.CompilerParams(vmem_limit_bytes=LIMIT)


def cost(us):
    return pl.CostEstimate(flops=int(us * 1.0e9), bytes_accessed=1 << 20, transcendentals=0)


def f32(*shape):
    return jax.ShapeDtypeStruct(shape, F32)


def edges_kernel(odd_ref, v_ref, after_ref, far_out, near_out, sems):
    rows = v_ref.shape[1]
    odd = odd_ref[0]
    copies = []
    for k, (side, dst) in enumerate(((odd, far_out), (1 - odd, near_out))):
        count = dst.shape[1]
        here = pl.ds(pl.multiple_of(side * (rows - count), EDGE), count)
        copies.append(pltpu.make_async_copy(v_ref.at[:, here, :], dst, sems.at[k]))
    for c in copies:
        c.start()
    for c in copies:
        c.wait()


def edges(odd, v, after, far, near):
    depth, rows, columns = v.shape
    return pl.pallas_call(
        edges_kernel,
        out_shape=(f32(depth, far, columns), f32(depth, near, columns)),
        in_specs=[SM, VM, ANY],
        out_specs=[VM] * 2,
        scratch_shapes=[pltpu.SemaphoreType.DMA((2,))],
        compiler_params=params(),
        cost_estimate=cost(0.2),
        name="edges",
    )(odd, v, after)


def one_hot(count, at):
    tap = lax.broadcasted_iota(jnp.int32, (count, WIDE), 0)
    lane = lax.broadcasted_iota(jnp.int32, (count, WIDE), 1)
    return jnp.where(lane == (at(tap) + WIDE) % WIDE, 1.0, 0.0).astype(BF16)


def pick(parts_and_places):
    got = None
    for part, place in parts_and_places:
        term = jnp.dot(part, place, preferred_element_type=F32)
        got = term if got is None else got + term
    return got


def prep_kernel(depth, inner, row_ref, col_ref, p_ref, *refs):
    outs, sums_ref, bases = refs[:6], refs[6], refs[7:]
    sums_ref[...] = jnp.zeros_like(sums_ref)
    for o in range(depth):
        sums_ref[2:3, :] += folded(p_ref[o] * p_ref[o])
    count = row_ref.shape[1]
    last = count - 1
    row_hi, row_lo = split(row_ref[...])
    col_hi, col_lo = split(col_ref[...])
    window = LANE + 2 * EDGE
    lane = lax.broadcasted_iota(jnp.int32, (window, WIDE), 1)
    for adjoint in (False, True):
        r_early, r_late, c_out = outs[3:] if adjoint else outs[:3]
        tall = EDGE if adjoint else 2 * EDGE
        turn = (lambda a: last - a) if adjoint else (lambda a: a)
        for base, gap in ((bases[0], inner + 2 * EDGE), (bases[1], tall + 2 * EDGE)):
            base[...] = pick((
                (row_hi, one_hot(count, turn)),
                (row_hi, one_hot(count, lambda a: turn(a) + gap)),
                (row_lo, one_hot(count, lambda a: turn(a) + 2 * gap)),
            ))
        bases[2][...] = pick(((col_hi, one_hot(count, lambda a: -turn(a))),))
        bases[3][...] = pick(((col_lo, one_hot(count, lambda a: LANE - turn(a))),))

        def banded(base, pair, rows, shift):
            wide = jnp.broadcast_to(base[pl.ds(pair, 1), :], (rows, WIDE))
            return pltpu.roll(wide, shift, 1, stride=1, stride_axis=0)

        for o in range(depth):
            for s in range(depth):
                pair = s * depth + o if adjoint else o * depth + s
                r_early[s, o * inner:(o + 1) * inner, :] = banded(bases[0], pair, inner, 1).astype(BF16)
                r_late[s, o * tall:(o + 1) * tall, :] = banded(bases[1], pair, tall, 1).astype(BF16)
                band = jnp.where(lane < LANE, banded(bases[2], pair, window, 0), banded(bases[3], pair, window, 0))
                c_out[o, s * WIDE:s * WIDE + window, :] = band.astype(BF16)
                c_out[o, s * WIDE + window:(s + 1) * WIDE, :] = jnp.zeros((WIDE - window, WIDE), BF16)


def prep(row, col, inner, direction):
    depth, _, count = row.shape
    pairs = depth * depth

    def bands(tall):
        return (
            jax.ShapeDtypeStruct((depth, depth * inner, WIDE), BF16),
            jax.ShapeDtypeStruct((depth, depth * tall, WIDE), BF16),
            jax.ShapeDtypeStruct((depth, depth * WIDE, WIDE), BF16),
        )

    return pl.pallas_call(
        functools.partial(prep_kernel, depth, inner),
        out_shape=bands(2 * EDGE) + bands(EDGE) + (f32(8, LANE),),
        in_specs=[VM] * 3,
        out_specs=[VM] * 7,
        scratch_shapes=[pltpu.VMEM((pairs, WIDE), F32)] * 4,
        compiler_params=params(),
        cost_estimate=cost(1.5),
        name="prep",
    )(row.reshape(pairs, count), col.reshape(pairs, count), direction)


def shifted(x, border):
    wide = jnp.concatenate([x, jnp.zeros((x.shape[0], LANE), F32)], axis=1)
    return split(pltpu.roll(wide, border, 1))


def put(win, at, group, hi, lo):
    rows = hi.shape[0]
    for g, part in enumerate((hi, lo, hi)):
        win[pl.ds(pl.multiple_of(at + g * group, EDGE), rows), :] = part


def along_rows(r_ref, win, v_hi, v_lo, s, group):
    if 3 * group < WIDE:
        win[s, 3 * group:, :] = jnp.zeros((WIDE - 3 * group, win.shape[2]), BF16)
    got = jnp.dot(r_ref[s], win[s], preferred_element_type=F32)
    v_hi[s], v_lo[s] = split(got)


def along_columns(sources, c_ref, o, rows, columns, depth):
    tall = []
    blocks = columns // LANE
    for pair in sources:
        for part in pair:
            for n in range(blocks):
                tall.append(jnp.concatenate(
                    [part[s, o * rows:(o + 1) * rows, n * LANE:n * LANE + WIDE] for s in range(depth)], axis=1))
    got = jnp.dot(jnp.concatenate(tall, axis=0), c_ref[o], preferred_element_type=F32)
    planes = []
    for k in range(len(sources)):
        out = []
        for n in range(blocks):
            at = (2 * k * blocks + n) * rows
            top, low = got[at:at + rows], got[at + blocks * rows:at + (blocks + 1) * rows]
            out.append(top[:, :LANE] + (top[:, LANE:] + low[:, :LANE]))
        planes.append(jnp.concatenate(out, axis=1))
    return planes


def folded(x):
    part = jnp.sum(x.reshape(x.shape[0] // 8, 8, x.shape[1]), axis=0)
    part = sum(part[:, n:n + LANE] for n in range(0, x.shape[1], LANE))
    return jnp.sum(part, axis=0, keepdims=True)


def early_kernel(border, odd_ref, v_ref, near_ref, r_ref, c_ref, out_ref, win, v_hi, v_lo):
    depth, rows, columns = v_ref.shape
    inner = rows - EDGE
    group = rows + EDGE
    odd = odd_ref[0]
    for s in range(depth):
        put(win.at[s], odd * EDGE, group, *shifted(v_ref[s], border))
        put(win.at[s], (1 - odd) * rows, group, *shifted(near_ref[s], border))
        along_rows(r_ref, win, v_hi, v_lo, s, group)
    for o in range(depth):
        out_ref[o], = along_columns(((v_hi, v_lo),), c_ref, o, inner, columns, depth)


def early(odd, v, near, r, c, border):
    depth, rows, columns = v.shape
    inner = rows - EDGE
    wide = columns + LANE
    return pl.pallas_call(
        functools.partial(early_kernel, border),
        out_shape=f32(depth, inner, columns),
        in_specs=[SM, VM, VM, VM, VM],
        out_specs=VM,
        scratch_shapes=[
            pltpu.VMEM((depth, WIDE, wide), BF16),
            pltpu.VMEM((depth, depth * inner, wide), BF16),
            pltpu.VMEM((depth, depth * inner, wide), BF16),
        ],
        compiler_params=params(),
        cost_estimate=cost(2.8),
        name="early",
    )(odd, v, near, r, c)


def late_rows(border, odd, v_ref, far_ref, r_ref, win, v_hi, v_lo):
    depth, rows, _ = v_ref.shape
    beyond = far_ref.shape[1]
    group = beyond + 2 * EDGE
    start = pl.multiple_of(odd * (rows - 2 * EDGE), EDGE)
    for s in range(depth):
        put(win.at[s], (1 - odd) * beyond, group, *shifted(v_ref[s, pl.ds(start, 2 * EDGE), :], border))
        put(win.at[s], odd * 2 * EDGE, group, *shifted(far_ref[s], border))
        along_rows(r_ref, win, v_hi, v_lo, s, group)


def late_scratch(depth, columns, tall):
    wide = columns + LANE
    return [
        pltpu.VMEM((depth, WIDE, wide), BF16),
        pltpu.VMEM((depth, depth * tall, wide), BF16),
        pltpu.VMEM((depth, depth * tall, wide), BF16),
    ]


def image_kernel(border, odd_ref, more_ref, v_ref, far_ref, r_ref, c_ref, in_ref, grad_ref, before_ref, after_ref, out_ref, beyond_ref, sums_ref, win, v_hi, v_lo):
    depth, rows, columns = v_ref.shape
    inner = rows - EDGE
    odd = odd_ref[0]
    more = more_ref[0]
    late_rows(border, odd, v_ref, far_ref, r_ref, win, v_hi, v_lo)
    sums_ref[...] = before_ref[...]
    for o in range(depth):
        both, = along_columns(((v_hi, v_lo),), c_ref, o, 2 * EDGE, columns, depth)
        first, second = both[:EDGE], both[EDGE:]
        edge = jnp.where(odd == 1, first, second)
        beyond_ref[o] = jnp.where(more == 1, jnp.where(odd == 1, second, first), 0.0)
        out_ref[o, pl.ds(pl.multiple_of(odd * inner, EDGE), EDGE), :] = edge
        out_ref[o, pl.ds(pl.multiple_of((1 - odd) * EDGE, EDGE), inner), :] = in_ref[o]
        sums_ref[0:1, :] += folded(grad_ref[o] * grad_ref[o])
        sums_ref[1:2, :] += folded(in_ref[o] * in_ref[o]) + folded(edge * edge)


def image_late(odd, more, v, far, r, c, inside, grad, before, after, border):
    depth, rows, columns = v.shape
    return pl.pallas_call(
        functools.partial(image_kernel, border),
        out_shape=(f32(depth, rows, columns), f32(depth, EDGE, columns), f32(8, LANE)),
        in_specs=[SM, SM] + [VM] * 7 + [ANY],
        out_specs=[VM] * 3,
        scratch_shapes=late_scratch(depth, columns, 2 * EDGE),
        compiler_params=params(),
        cost_estimate=cost(2.0),
        name="image_late",
    )(odd, more, v, far, r, c, inside, grad, before, after)


def last_kernel(border, odd_ref, damp_ref, res_ref, res_far_ref, g_in_ref, x_ref, f_ref, f_far_ref, h_in_ref, p_ref, r_ref, c_ref, before_ref,
                g_ref, h_ref, sums_ref, win, v_hi, v_lo, win2, v_hi2, v_lo2):
    depth, rows, columns = res_ref.shape
    inner = rows - EDGE
    odd = odd_ref[0]
    damp = damp_ref[0]
    late_rows(border, odd, res_ref, res_far_ref, r_ref, win, v_hi, v_lo)
    late_rows(border, odd, f_ref, f_far_ref, r_ref, win2, v_hi2, v_lo2)
    sums_ref[...] = before_ref[...]
    for o in range(depth):
        g_edge, h_edge = along_columns(((v_hi, v_lo), (v_hi2, v_lo2)), c_ref, o, EDGE, columns, depth)
        for at, count, g, h in (
            (pl.multiple_of(odd * inner, EDGE), EDGE, g_edge, h_edge),
            (pl.multiple_of((1 - odd) * EDGE, EDGE), inner, g_in_ref[o], h_in_ref[o]),
        ):
            here = pl.ds(at, count)
            g = g - damp * x_ref[o, here, :]
            h = h + damp * p_ref[o, here, :]
            g_ref[o, here, :] = g
            h_ref[o, here, :] = h
            sums_ref[3:4, :] += folded(g * g)
            sums_ref[4:5, :] += folded(g * h)
            sums_ref[5:6, :] += folded(h * h)


def last_late(odd, damp, res, res_far, g_in, x, image, image_far, h_in, p, r, c, before, border):
    depth, rows, columns = res.shape
    return pl.pallas_call(
        functools.partial(last_kernel, border),
        out_shape=(f32(depth, rows, columns), f32(depth, rows, columns), f32(8, LANE)),
        in_specs=[SM, SM] + [VM] * 11,
        out_specs=[VM] * 3,
        scratch_shapes=late_scratch(depth, columns, EDGE) * 2,
        compiler_params=params(),
        cost_estimate=cost(2.6),
        name="last_late",
    )(odd, damp, res, res_far, g_in, x, image, image_far, h_in, p, r, c, before)


def final_kernel(damp_ref, mine_ref, other_ref, x_ref, r_ref, p_ref, f_ref, g_ref, h_ref,
                 nx_out, nr_out, ng_out, np_out, nx, nr, ng, nd, sems):
    depth = x_ref.shape[0]
    damp = damp_ref[0]
    sums = jnp.sum(mine_ref[...] + other_ref[...], axis=1, keepdims=True)
    before, image, direction, gg, gh, hh = (sums[k:k + 1, :] for k in range(6))
    step = before / (image + damp * direction)
    after = gg - step * (2.0 * gh - step * hh)
    ratio = after / before
    copies = []
    for o in range(depth):
        p = p_ref[o]
        new = g_ref[o] - step * h_ref[o]
        for k, (buf, out, value) in enumerate((
            (nx, nx_out, x_ref[o] + step * p),
            (nr, nr_out, r_ref[o] - step * f_ref[o]),
            (ng, ng_out, new),
            (nd, np_out, new + ratio * p),
        )):
            buf[o] = value
            copies.append(pltpu.make_async_copy(buf.at[o], out.at[o], sems.at[o, k]))
            copies[-1].start()
    for c in copies:
        c.wait()


def final(damp, mine, other, x, r, p, f, g, h):
    shape = x.shape
    return pl.pallas_call(
        final_kernel,
        out_shape=(f32(*shape),) * 4,
        in_specs=[SM] + [VM] * 8,
        out_specs=[ANY] * 4,
        scratch_shapes=[pltpu.VMEM(shape, F32)] * 4 + [pltpu.SemaphoreType.DMA((shape[0], 4))],
        compiler_params=params(),
        cost_estimate=cost(2.0),
        name="final",
    )(damp, mine, other, x, r, p, f, g, h)


def swap(values, axis, step):
    return lax.ppermute(values, axis, [(i, i ^ step) for i in range(lax.axis_size(axis))])


def body(solution, residual, gradient, direction, row_taps, col_taps, damping):
    border = row_taps.shape[2] // 2
    depth, rows, columns = direction.shape
    inner = rows - EDGE
    peers = lax.axis_size("lat")
    odd = lax.axis_index("lat") % 2
    odd_arr = jnp.full((1,), odd, jnp.int32)
    far_pairs = [p for a in range(1, peers - 1, 2) for p in ((a, a + 1), (a + 1, a))]

    def near_swap(v):
        return swap(v, "lat", 1)

    def far_swap(v):
        return lax.ppermute(v, "lat", far_pairs)

    place = lax.axis_index("lat")
    more = jnp.full((1,), jnp.where(odd == 1, place < peers - 1, place > 0), jnp.int32)

    p_far_edge, p_near_edge = edges(odd_arr, direction, odd_arr, 2 * EDGE, EDGE)
    p_far, p_near = far_swap(p_far_edge), near_swap(p_near_edge)
    re, rl, c, rae, ral, ca, sums = prep(row_taps, col_taps, inner, direction)

    r_far_edge = lax.dynamic_slice_in_dim(residual, odd * inner, EDGE, axis=1)
    r_near_edge = lax.dynamic_slice_in_dim(residual, (1 - odd) * inner, EDGE, axis=1)
    p_near, r_near_edge = lax.optimization_barrier((p_near, r_near_edge))
    r_near = near_swap(r_near_edge)
    image_in = early(odd_arr, direction, p_near, re, c, border)
    f_near = near_swap(lax.dynamic_slice_in_dim(image_in, (1 - odd) * (inner - EDGE), EDGE, axis=1))
    g_in = early(odd_arr, residual, r_near, rae, ca, border)
    g_in, r_far_edge = lax.optimization_barrier((g_in, r_far_edge))
    r_far = far_swap(r_far_edge)
    image, f_far, sums = image_late(odd_arr, more, direction, p_far, rl, c, image_in, gradient, sums, g_in, border)
    h_in = early(odd_arr, image, f_near, rae, ca, border)
    g, h, sums = last_late(odd_arr, damping, residual, r_far, g_in, solution, image, f_far, h_in, direction, ral, ca, sums, border)

    step = 1
    while 2 * step < peers:
        sums = sums + swap(sums, "lat", step)
        step *= 2
    other = swap(sums, "lat", step)
    return final(damping, sums, other, solution, residual, direction, image, g, h)


def solution(mesh):
    split_rows = P("stack", "lat", None)
    return jax.shard_map(
        body,
        mesh=mesh,
        in_specs=(split_rows,) * 4 + (P(),) * 3,
        out_specs=(split_rows,) * 4,
        check_vma=False,
    )
```

```python
import functools

import jax
import jax.numpy as jnp
from jax import lax
from jax.experimental import pallas as pl
from jax.experimental.pallas import tpu as pltpu
from jax.sharding import PartitionSpec as P

F32 = jnp.float32
BF16 = jnp.bfloat16
EDGE = 16
LANE = 128
WIDE = 256
VM = pl.BlockSpec(memory_space=pltpu.VMEM)
SM = pl.BlockSpec(memory_space=pltpu.SMEM)
ANY = pl.BlockSpec(memory_space=pl.ANY)
LIMIT = 20 * 2**20


def split(x):
    hi = x.astype(BF16)
    return hi, (x - hi.astype(F32)).astype(BF16)


def params():
    return pltpu.CompilerParams(vmem_limit_bytes=LIMIT)


def cost(us):
    return pl.CostEstimate(flops=int(us * 1.0e9), bytes_accessed=1 << 20, transcendentals=0)


def f32(*shape):
    return jax.ShapeDtypeStruct(shape, F32)


def edges_kernel(odd_ref, v_ref, after_ref, far_out, near_out, sems):
    rows = v_ref.shape[1]
    odd = odd_ref[0]
    copies = []
    for k, (side, dst) in enumerate(((odd, far_out), (1 - odd, near_out))):
        count = dst.shape[1]
        here = pl.ds(pl.multiple_of(side * (rows - count), EDGE), count)
        copies.append(pltpu.make_async_copy(v_ref.at[:, here, :], dst, sems.at[k]))
    for c in copies:
        c.start()
    for c in copies:
        c.wait()


def edges(odd, v, after, far, near):
    depth, rows, columns = v.shape
    return pl.pallas_call(
        edges_kernel,
        out_shape=(f32(depth, far, columns), f32(depth, near, columns)),
        in_specs=[SM, VM, ANY],
        out_specs=[VM] * 2,
        scratch_shapes=[pltpu.SemaphoreType.DMA((2,))],
        compiler_params=params(),
        cost_estimate=cost(0.2),
        name="edges",
    )(odd, v, after)


def one_hot(count, at):
    tap = lax.broadcasted_iota(jnp.int32, (count, WIDE), 0)
    lane = lax.broadcasted_iota(jnp.int32, (count, WIDE), 1)
    return jnp.where(lane == (at(tap) + WIDE) % WIDE, 1.0, 0.0).astype(BF16)


def pick(parts_and_places):
    got = None
    for part, place in parts_and_places:
        term = jnp.dot(part, place, preferred_element_type=F32)
        got = term if got is None else got + term
    return got


def prep_kernel(depth, inner, row_ref, col_ref, p_ref, *refs):
    outs, sums_ref, bases = refs[:6], refs[6], refs[7:]
    sums_ref[...] = jnp.zeros_like(sums_ref)
    for o in range(depth):
        sums_ref[2:3, :] += folded(p_ref[o] * p_ref[o])
    count = row_ref.shape[1]
    last = count - 1
    row_hi, row_lo = split(row_ref[...])
    col_hi, col_lo = split(col_ref[...])
    window = LANE + 2 * EDGE
    lane = lax.broadcasted_iota(jnp.int32, (window, WIDE), 1)
    back = lax.broadcasted_iota(jnp.int32, (window, WIDE), 0) - jnp.where(lane < LANE, lane, lane - LANE)
    inside = (back >= 0) & (back <= last)
    for adjoint in (False, True):
        r_early, r_late, c_out = outs[3:] if adjoint else outs[:3]
        tall = EDGE if adjoint else 2 * EDGE
        turn = (lambda a: last - a) if adjoint else (lambda a: a)
        for base, gap in ((bases[0], inner + 2 * EDGE), (bases[1], tall + 2 * EDGE)):
            base[...] = pick((
                (row_hi, one_hot(count, turn)),
                (row_hi, one_hot(count, lambda a: turn(a) + gap)),
                (row_lo, one_hot(count, lambda a: turn(a) + 2 * gap)),
            ))
        bases[2][...] = pick(((col_hi, one_hot(count, lambda a: -turn(a))), (col_lo, one_hot(count, lambda a: LANE - turn(a)))))

        def banded(base, pair, rows, shift):
            wide = jnp.broadcast_to(base[pl.ds(pair, 1), :], (rows, WIDE))
            return pltpu.roll(wide, shift, 1, stride=1, stride_axis=0)

        for o in range(depth):
            for s in range(depth):
                pair = s * depth + o if adjoint else o * depth + s
                r_early[s, o * inner:(o + 1) * inner, :] = banded(bases[0], pair, inner, 1).astype(BF16)
                r_late[s, o * tall:(o + 1) * tall, :] = banded(bases[1], pair, tall, 1).astype(BF16)
                band = jnp.where(inside, banded(bases[2], pair, window, 0), 0.0)
                c_out[o, s * WIDE:s * WIDE + window, :] = band.astype(BF16)
                c_out[o, s * WIDE + window:(s + 1) * WIDE, :] = jnp.zeros((WIDE - window, WIDE), BF16)


def prep(row, col, inner, direction):
    depth, _, count = row.shape
    pairs = depth * depth

    def bands(tall):
        return (
            jax.ShapeDtypeStruct((depth, depth * inner, WIDE), BF16),
            jax.ShapeDtypeStruct((depth, depth * tall, WIDE), BF16),
            jax.ShapeDtypeStruct((depth, depth * WIDE, WIDE), BF16),
        )

    return pl.pallas_call(
        functools.partial(prep_kernel, depth, inner),
        out_shape=bands(2 * EDGE) + bands(EDGE) + (f32(8, LANE),),
        in_specs=[VM] * 3,
        out_specs=[VM] * 7,
        scratch_shapes=[pltpu.VMEM((pairs, WIDE), F32)] * 3,
        compiler_params=params(),
        cost_estimate=cost(1.5),
        name="prep",
    )(row.reshape(pairs, count), col.reshape(pairs, count), direction)


def shifted(x, border):
    wide = jnp.concatenate([x, jnp.zeros((x.shape[0], LANE), F32)], axis=1)
    return split(pltpu.roll(wide, border, 1))


def put(win, at, group, hi, lo):
    rows = hi.shape[0]
    for g, part in enumerate((hi, lo, hi)):
        win[pl.ds(pl.multiple_of(at + g * group, EDGE), rows), :] = part


def along_rows(r_ref, win, v_hi, v_lo, s, group):
    if 3 * group < WIDE:
        win[s, 3 * group:, :] = jnp.zeros((WIDE - 3 * group, win.shape[2]), BF16)
    got = jnp.dot(r_ref[s], win[s], preferred_element_type=F32)
    v_hi[s], v_lo[s] = split(got)


def along_columns(sources, c_ref, o, rows, columns, depth):
    tall = []
    blocks = columns // LANE
    for pair in sources:
        for part in pair:
            for n in range(blocks):
                tall.append(jnp.concatenate(
                    [part[s, o * rows:(o + 1) * rows, n * LANE:n * LANE + WIDE] for s in range(depth)], axis=1))
    got = jnp.dot(jnp.concatenate(tall, axis=0), c_ref[o], preferred_element_type=F32)
    planes = []
    for k in range(len(sources)):
        out = []
        for n in range(blocks):
            at = (2 * k * blocks + n) * rows
            top, low = got[at:at + rows], got[at + blocks * rows:at + (blocks + 1) * rows]
            out.append(top[:, :LANE] + (top[:, LANE:] + low[:, :LANE]))
        planes.append(jnp.concatenate(out, axis=1))
    return planes


def folded(x):
    part = jnp.sum(x.reshape(x.shape[0] // 8, 8, x.shape[1]), axis=0)
    part = sum(part[:, n:n + LANE] for n in range(0, x.shape[1], LANE))
    return jnp.sum(part, axis=0, keepdims=True)


def early_kernel(border, odd_ref, v_ref, near_ref, r_ref, c_ref, out_ref, win, v_hi, v_lo):
    depth, rows, columns = v_ref.shape
    inner = rows - EDGE
    group = rows + EDGE
    odd = odd_ref[0]
    for s in range(depth):
        put(win.at[s], odd * EDGE, group, *shifted(v_ref[s], border))
        put(win.at[s], (1 - odd) * rows, group, *shifted(near_ref[s], border))
        along_rows(r_ref, win, v_hi, v_lo, s, group)
    for o in range(depth):
        out_ref[o], = along_columns(((v_hi, v_lo),), c_ref, o, inner, columns, depth)


def early(odd, v, near, r, c, border):
    depth, rows, columns = v.shape
    inner = rows - EDGE
    wide = columns + LANE
    return pl.pallas_call(
        functools.partial(early_kernel, border),
        out_shape=f32(depth, inner, columns),
        in_specs=[SM, VM, VM, VM, VM],
        out_specs=VM,
        scratch_shapes=[
            pltpu.VMEM((depth, WIDE, wide), BF16),
            pltpu.VMEM((depth, depth * inner, wide), BF16),
            pltpu.VMEM((depth, depth * inner, wide), BF16),
        ],
        compiler_params=params(),
        cost_estimate=cost(2.8),
        name="early",
    )(odd, v, near, r, c)


def late_rows(border, odd, v_ref, far_ref, r_ref, win, v_hi, v_lo):
    depth, rows, _ = v_ref.shape
    beyond = far_ref.shape[1]
    group = beyond + 2 * EDGE
    start = pl.multiple_of(odd * (rows - 2 * EDGE), EDGE)
    for s in range(depth):
        put(win.at[s], (1 - odd) * beyond, group, *shifted(v_ref[s, pl.ds(start, 2 * EDGE), :], border))
        put(win.at[s], odd * 2 * EDGE, group, *shifted(far_ref[s], border))
        along_rows(r_ref, win, v_hi, v_lo, s, group)


def late_scratch(depth, columns, tall):
    wide = columns + LANE
    return [
        pltpu.VMEM((depth, WIDE, wide), BF16),
        pltpu.VMEM((depth, depth * tall, wide), BF16),
        pltpu.VMEM((depth, depth * tall, wide), BF16),
    ]


def image_kernel(border, odd_ref, more_ref, v_ref, far_ref, r_ref, c_ref, in_ref, grad_ref, before_ref, after_ref, out_ref, beyond_ref, sums_ref, win, v_hi, v_lo):
    depth, rows, columns = v_ref.shape
    inner = rows - EDGE
    odd = odd_ref[0]
    more = more_ref[0]
    late_rows(border, odd, v_ref, far_ref, r_ref, win, v_hi, v_lo)
    sums_ref[...] = before_ref[...]
    for o in range(depth):
        both, = along_columns(((v_hi, v_lo),), c_ref, o, 2 * EDGE, columns, depth)
        first, second = both[:EDGE], both[EDGE:]
        edge = jnp.where(odd == 1, first, second)
        beyond_ref[o] = jnp.where(more == 1, jnp.where(odd == 1, second, first), 0.0)
        out_ref[o, pl.ds(pl.multiple_of(odd * inner, EDGE), EDGE), :] = edge
        out_ref[o, pl.ds(pl.multiple_of((1 - odd) * EDGE, EDGE), inner), :] = in_ref[o]
        sums_ref[0:1, :] += folded(grad_ref[o] * grad_ref[o])
        sums_ref[1:2, :] += folded(in_ref[o] * in_ref[o]) + folded(edge * edge)


def image_late(odd, more, v, far, r, c, inside, grad, before, after, border):
    depth, rows, columns = v.shape
    return pl.pallas_call(
        functools.partial(image_kernel, border),
        out_shape=(f32(depth, rows, columns), f32(depth, EDGE, columns), f32(8, LANE)),
        in_specs=[SM, SM] + [VM] * 7 + [ANY],
        out_specs=[VM] * 3,
        scratch_shapes=late_scratch(depth, columns, 2 * EDGE),
        compiler_params=params(),
        cost_estimate=cost(2.0),
        name="image_late",
    )(odd, more, v, far, r, c, inside, grad, before, after)


def last_kernel(border, odd_ref, damp_ref, res_ref, res_far_ref, g_in_ref, x_ref, f_ref, f_far_ref, h_in_ref, p_ref, r_ref, c_ref, before_ref,
                g_ref, h_ref, sums_ref, win, v_hi, v_lo, win2, v_hi2, v_lo2):
    depth, rows, columns = res_ref.shape
    inner = rows - EDGE
    odd = odd_ref[0]
    damp = damp_ref[0]
    late_rows(border, odd, res_ref, res_far_ref, r_ref, win, v_hi, v_lo)
    late_rows(border, odd, f_ref, f_far_ref, r_ref, win2, v_hi2, v_lo2)
    sums_ref[...] = before_ref[...]
    for o in range(depth):
        g_edge, h_edge = along_columns(((v_hi, v_lo), (v_hi2, v_lo2)), c_ref, o, EDGE, columns, depth)
        for at, count, g, h in (
            (pl.multiple_of(odd * inner, EDGE), EDGE, g_edge, h_edge),
            (pl.multiple_of((1 - odd) * EDGE, EDGE), inner, g_in_ref[o], h_in_ref[o]),
        ):
            here = pl.ds(at, count)
            g = g - damp * x_ref[o, here, :]
            h = h + damp * p_ref[o, here, :]
            g_ref[o, here, :] = g
            h_ref[o, here, :] = h
            sums_ref[3:4, :] += folded(g * g)
            sums_ref[4:5, :] += folded(g * h)
            sums_ref[5:6, :] += folded(h * h)


def last_late(odd, damp, res, res_far, g_in, x, image, image_far, h_in, p, r, c, before, border):
    depth, rows, columns = res.shape
    return pl.pallas_call(
        functools.partial(last_kernel, border),
        out_shape=(f32(depth, rows, columns), f32(depth, rows, columns), f32(8, LANE)),
        in_specs=[SM, SM] + [VM] * 11,
        out_specs=[VM] * 3,
        scratch_shapes=late_scratch(depth, columns, EDGE) * 2,
        compiler_params=params(),
        cost_estimate=cost(2.6),
        name="last_late",
    )(odd, damp, res, res_far, g_in, x, image, image_far, h_in, p, r, c, before)


def final_kernel(damp_ref, mine_ref, other_ref, x_ref, r_ref, p_ref, f_ref, g_ref, h_ref,
                 nx_out, nr_out, ng_out, np_out, nx, nr, ng, nd, sems):
    depth = x_ref.shape[0]
    damp = damp_ref[0]
    sums = jnp.sum(mine_ref[...] + other_ref[...], axis=1, keepdims=True)
    before, image, direction, gg, gh, hh = (sums[k:k + 1, :] for k in range(6))
    step = before / (image + damp * direction)
    after = gg - step * (2.0 * gh - step * hh)
    ratio = after / before
    copies = []
    for o in range(depth):
        p = p_ref[o]
        new = g_ref[o] - step * h_ref[o]
        for k, (buf, out, value) in enumerate((
            (nx, nx_out, x_ref[o] + step * p),
            (nr, nr_out, r_ref[o] - step * f_ref[o]),
            (ng, ng_out, new),
            (nd, np_out, new + ratio * p),
        )):
            buf[o] = value
            copies.append(pltpu.make_async_copy(buf.at[o], out.at[o], sems.at[o, k]))
            copies[-1].start()
    for c in copies:
        c.wait()


def final(damp, mine, other, x, r, p, f, g, h):
    shape = x.shape
    return pl.pallas_call(
        final_kernel,
        out_shape=(f32(*shape),) * 4,
        in_specs=[SM] + [VM] * 8,
        out_specs=[ANY] * 4,
        scratch_shapes=[pltpu.VMEM(shape, F32)] * 4 + [pltpu.SemaphoreType.DMA((shape[0], 4))],
        compiler_params=params(),
        cost_estimate=cost(2.0),
        name="final",
    )(damp, mine, other, x, r, p, f, g, h)


def swap(values, axis, step):
    return lax.ppermute(values, axis, [(i, i ^ step) for i in range(lax.axis_size(axis))])


def body(solution, residual, gradient, direction, row_taps, col_taps, damping):
    border = row_taps.shape[2] // 2
    depth, rows, columns = direction.shape
    inner = rows - EDGE
    peers = lax.axis_size("lat")
    odd = lax.axis_index("lat") % 2
    odd_arr = jnp.full((1,), odd, jnp.int32)
    far_pairs = [p for a in range(1, peers - 1, 2) for p in ((a, a + 1), (a + 1, a))]

    def near_swap(v):
        return swap(v, "lat", 1)

    def far_swap(v):
        return lax.ppermute(v, "lat", far_pairs)

    place = lax.axis_index("lat")
    more = jnp.full((1,), jnp.where(odd == 1, place < peers - 1, place > 0), jnp.int32)

    p_far_edge, p_near_edge = edges(odd_arr, direction, odd_arr, 2 * EDGE, EDGE)
    p_far, p_near = far_swap(p_far_edge), near_swap(p_near_edge)
    re, rl, c, rae, ral, ca, sums = prep(row_taps, col_taps, inner, direction)

    r_far_edge = lax.dynamic_slice_in_dim(residual, odd * inner, EDGE, axis=1)
    r_near_edge = lax.dynamic_slice_in_dim(residual, (1 - odd) * inner, EDGE, axis=1)
    p_near, r_near_edge = lax.optimization_barrier((p_near, r_near_edge))
    r_near = near_swap(r_near_edge)
    image_in = early(odd_arr, direction, p_near, re, c, border)
    f_near = near_swap(lax.dynamic_slice_in_dim(image_in, (1 - odd) * (inner - EDGE), EDGE, axis=1))
    g_in = early(odd_arr, residual, r_near, rae, ca, border)
    g_in, r_far_edge = lax.optimization_barrier((g_in, r_far_edge))
    r_far = far_swap(r_far_edge)
    image, f_far, sums = image_late(odd_arr, more, direction, p_far, rl, c, image_in, gradient, sums, g_in, border)
    h_in = early(odd_arr, image, f_near, rae, ca, border)
    g, h, sums = last_late(odd_arr, damping, residual, r_far, g_in, solution, image, f_far, h_in, direction, ral, ca, sums, border)

    step = 1
    while 2 * step < peers:
        sums = sums + swap(sums, "lat", step)
        step *= 2
    other = swap(sums, "lat", step)
    return final(damping, sums, other, solution, residual, direction, image, g, h)


def solution(mesh):
    split_rows = P("stack", "lat", None)
    return jax.shard_map(
        body,
        mesh=mesh,
        in_specs=(split_rows,) * 4 + (P(),) * 3,
        out_specs=(split_rows,) * 4,
        check_vma=False,
    )
```

```python
import functools

import jax
import jax.numpy as jnp
from jax import lax
from jax.experimental import pallas as pl
from jax.experimental.pallas import tpu as pltpu
from jax.sharding import PartitionSpec as P

F32 = jnp.float32
BF16 = jnp.bfloat16
EDGE = 16
LANE = 128
WIDE = 256
VM = pl.BlockSpec(memory_space=pltpu.VMEM)
SM = pl.BlockSpec(memory_space=pltpu.SMEM)
ANY = pl.BlockSpec(memory_space=pl.ANY)
LIMIT = 20 * 2**20


def split(x):
    hi = x.astype(BF16)
    return hi, (x - hi.astype(F32)).astype(BF16)


def params():
    return pltpu.CompilerParams(vmem_limit_bytes=LIMIT)


def cost(us):
    return pl.CostEstimate(flops=int(us * 1.0e9), bytes_accessed=1 << 20, transcendentals=0)


def f32(*shape):
    return jax.ShapeDtypeStruct(shape, F32)


def edges_kernel(odd_ref, v_ref, after_ref, far_out, near_out, sems):
    rows = v_ref.shape[1]
    odd = odd_ref[0]
    copies = []
    for k, (side, dst) in enumerate(((odd, far_out), (1 - odd, near_out))):
        count = dst.shape[1]
        here = pl.ds(pl.multiple_of(side * (rows - count), EDGE), count)
        copies.append(pltpu.make_async_copy(v_ref.at[:, here, :], dst, sems.at[k]))
    for c in copies:
        c.start()
    for c in copies:
        c.wait()


def edges(odd, v, after, far, near):
    depth, rows, columns = v.shape
    return pl.pallas_call(
        edges_kernel,
        out_shape=(f32(depth, far, columns), f32(depth, near, columns)),
        in_specs=[SM, VM, ANY],
        out_specs=[VM] * 2,
        scratch_shapes=[pltpu.SemaphoreType.DMA((2,))],
        compiler_params=params(),
        cost_estimate=cost(0.2),
        name="edges",
    )(odd, v, after)


def one_hot(count, at):
    tap = lax.broadcasted_iota(jnp.int32, (count, WIDE), 0)
    lane = lax.broadcasted_iota(jnp.int32, (count, WIDE), 1)
    return jnp.where(lane == (at(tap) + WIDE) % WIDE, 1.0, 0.0).astype(BF16)


def pick(parts_and_places):
    got = None
    for part, place in parts_and_places:
        term = jnp.dot(part, place, preferred_element_type=F32)
        got = term if got is None else got + term
    return got


def prep_kernel(depth, inner, row_ref, col_ref, p_ref, *refs):
    outs, sums_ref, bases = refs[:6], refs[6], refs[7:]
    sums_ref[...] = jnp.zeros_like(sums_ref)
    for o in range(depth):
        sums_ref[2:3, :] += folded(p_ref[o] * p_ref[o])
    count = row_ref.shape[1]
    last = count - 1
    row_hi, row_lo = split(row_ref[...])
    col_hi, col_lo = split(col_ref[...])
    window = LANE + 2 * EDGE
    lane = lax.broadcasted_iota(jnp.int32, (window, WIDE), 1)
    back = lax.broadcasted_iota(jnp.int32, (window, WIDE), 0) - jnp.where(lane < LANE, lane, lane - LANE)
    inside = (back >= 0) & (back <= last)
    for adjoint in (False, True):
        r_early, r_late, c_out = outs[3:] if adjoint else outs[:3]
        tall = EDGE if adjoint else 2 * EDGE
        turn = (lambda a: last - a) if adjoint else (lambda a: a)
        for base, gap in ((bases[0], inner + 2 * EDGE), (bases[1], tall + 2 * EDGE)):
            base[...] = pick((
                (row_hi, one_hot(count, turn)),
                (row_hi, one_hot(count, lambda a: turn(a) + gap)),
                (row_lo, one_hot(count, lambda a: turn(a) + 2 * gap)),
            ))
        bases[2][...] = pick(((col_hi, one_hot(count, lambda a: -turn(a))), (col_lo, one_hot(count, lambda a: LANE - turn(a)))))

        def banded(base, pair, rows, shift):
            wide = jnp.broadcast_to(base[pl.ds(pair, 1), :], (rows, WIDE))
            return pltpu.roll(wide, shift, 1, stride=1, stride_axis=0)

        for o in range(depth):
            for s in range(depth):
                pair = s * depth + o if adjoint else o * depth + s
                r_early[s, o * inner:(o + 1) * inner, :] = banded(bases[0], pair, inner, 1).astype(BF16)
                r_late[s, o * tall:(o + 1) * tall, :] = banded(bases[1], pair, tall, 1).astype(BF16)
                band = jnp.where(inside, banded(bases[2], pair, window, 0), 0.0)
                c_out[o, s * WIDE:s * WIDE + window, :] = band.astype(BF16)
                c_out[o, s * WIDE + window:(s + 1) * WIDE, :] = jnp.zeros((WIDE - window, WIDE), BF16)


def prep(row, col, inner, direction):
    depth, _, count = row.shape
    pairs = depth * depth

    def bands(tall):
        return (
            jax.ShapeDtypeStruct((depth, depth * inner, WIDE), BF16),
            jax.ShapeDtypeStruct((depth, depth * tall, WIDE), BF16),
            jax.ShapeDtypeStruct((depth, depth * WIDE, WIDE), BF16),
        )

    return pl.pallas_call(
        functools.partial(prep_kernel, depth, inner),
        out_shape=bands(2 * EDGE) + bands(EDGE) + (f32(8, LANE),),
        in_specs=[VM] * 3,
        out_specs=[VM] * 7,
        scratch_shapes=[pltpu.VMEM((pairs, WIDE), F32)] * 3,
        compiler_params=params(),
        cost_estimate=cost(1.5),
        name="prep",
    )(row.reshape(pairs, count), col.reshape(pairs, count), direction)


def shifted(x, border):
    wide = jnp.concatenate([x, jnp.zeros((x.shape[0], LANE), F32)], axis=1)
    return split(pltpu.roll(wide, border, 1))


def put(win, at, group, hi, lo):
    rows = hi.shape[0]
    for g, part in enumerate((hi, lo, hi)):
        win[pl.ds(pl.multiple_of(at + g * group, EDGE), rows), :] = part


def along_rows(r_ref, win, v_hi, v_lo, s, group):
    if 3 * group < WIDE:
        win[s, 3 * group:, :] = jnp.zeros((WIDE - 3 * group, win.shape[2]), BF16)
    got = jnp.dot(r_ref[s], win[s], preferred_element_type=F32)
    v_hi[s], v_lo[s] = split(got)


def along_columns(sources, c_ref, o, rows, columns, depth):
    tall = []
    blocks = columns // LANE
    for pair in sources:
        for part in pair:
            for n in range(blocks):
                tall.append(jnp.concatenate(
                    [part[s, o * rows:(o + 1) * rows, n * LANE:n * LANE + WIDE] for s in range(depth)], axis=1))
    got = jnp.dot(jnp.concatenate(tall, axis=0), c_ref[o], preferred_element_type=F32)
    planes = []
    for k in range(len(sources)):
        out = []
        for n in range(blocks):
            at = (2 * k * blocks + n) * rows
            top, low = got[at:at + rows], got[at + blocks * rows:at + (blocks + 1) * rows]
            out.append(top[:, :LANE] + (top[:, LANE:] + low[:, :LANE]))
        planes.append(jnp.concatenate(out, axis=1))
    return planes


def folded(x):
    part = jnp.sum(x.reshape(x.shape[0] // 8, 8, x.shape[1]), axis=0)
    part = sum(part[:, n:n + LANE] for n in range(0, x.shape[1], LANE))
    return jnp.sum(part, axis=0, keepdims=True)


def early_kernel(border, odd_ref, v_ref, near_ref, r_ref, c_ref, out_ref, win, v_hi, v_lo):
    depth, rows, columns = v_ref.shape
    inner = rows - EDGE
    group = rows + EDGE
    odd = odd_ref[0]
    for s in range(depth):
        put(win.at[s], odd * EDGE, group, *shifted(v_ref[s], border))
        put(win.at[s], (1 - odd) * rows, group, *shifted(near_ref[s], border))
        along_rows(r_ref, win, v_hi, v_lo, s, group)
    for o in range(depth):
        out_ref[o], = along_columns(((v_hi, v_lo),), c_ref, o, inner, columns, depth)


def early(odd, v, near, r, c, border):
    depth, rows, columns = v.shape
    inner = rows - EDGE
    wide = columns + LANE
    return pl.pallas_call(
        functools.partial(early_kernel, border),
        out_shape=f32(depth, inner, columns),
        in_specs=[SM, VM, VM, VM, VM],
        out_specs=VM,
        scratch_shapes=[
            pltpu.VMEM((depth, WIDE, wide), BF16),
            pltpu.VMEM((depth, depth * inner, wide), BF16),
            pltpu.VMEM((depth, depth * inner, wide), BF16),
        ],
        compiler_params=params(),
        cost_estimate=cost(2.8),
        name="early",
    )(odd, v, near, r, c)


def late_rows(border, odd, v_ref, far_ref, r_ref, win, v_hi, v_lo):
    depth, rows, _ = v_ref.shape
    beyond = far_ref.shape[1]
    group = beyond + 2 * EDGE
    start = pl.multiple_of(odd * (rows - 2 * EDGE), EDGE)
    for s in range(depth):
        put(win.at[s], (1 - odd) * beyond, group, *shifted(v_ref[s, pl.ds(start, 2 * EDGE), :], border))
        put(win.at[s], odd * 2 * EDGE, group, *shifted(far_ref[s], border))
        along_rows(r_ref, win, v_hi, v_lo, s, group)


def late_scratch(depth, columns, tall):
    wide = columns + LANE
    return [
        pltpu.VMEM((depth, WIDE, wide), BF16),
        pltpu.VMEM((depth, depth * tall, wide), BF16),
        pltpu.VMEM((depth, depth * tall, wide), BF16),
    ]


def image_kernel(border, odd_ref, more_ref, v_ref, far_ref, r_ref, c_ref, in_ref, grad_ref, before_ref, after_ref, out_ref, beyond_ref, sums_ref, win, v_hi, v_lo):
    depth, rows, columns = v_ref.shape
    inner = rows - EDGE
    odd = odd_ref[0]
    more = more_ref[0]
    late_rows(border, odd, v_ref, far_ref, r_ref, win, v_hi, v_lo)
    sums_ref[...] = before_ref[...]
    for o in range(depth):
        both, = along_columns(((v_hi, v_lo),), c_ref, o, 2 * EDGE, columns, depth)
        first, second = both[:EDGE], both[EDGE:]
        edge = jnp.where(odd == 1, first, second)
        beyond_ref[o] = jnp.where(more == 1, jnp.where(odd == 1, second, first), 0.0)
        out_ref[o, pl.ds(pl.multiple_of(odd * inner, EDGE), EDGE), :] = edge
        out_ref[o, pl.ds(pl.multiple_of((1 - odd) * EDGE, EDGE), inner), :] = in_ref[o]
        sums_ref[0:1, :] += folded(grad_ref[o] * grad_ref[o])
        sums_ref[1:2, :] += folded(in_ref[o] * in_ref[o]) + folded(edge * edge)


def image_late(odd, more, v, far, r, c, inside, grad, before, after, border):
    depth, rows, columns = v.shape
    return pl.pallas_call(
        functools.partial(image_kernel, border),
        out_shape=(f32(depth, rows, columns), f32(depth, EDGE, columns), f32(8, LANE)),
        in_specs=[SM, SM] + [VM] * 7 + [ANY],
        out_specs=[VM] * 3,
        scratch_shapes=late_scratch(depth, columns, 2 * EDGE),
        compiler_params=params(),
        cost_estimate=cost(2.0),
        name="image_late",
    )(odd, more, v, far, r, c, inside, grad, before, after)


def last_kernel(border, odd_ref, damp_ref, res_ref, res_far_ref, g_in_ref, x_ref, f_ref, f_far_ref, h_in_ref, p_ref, r_ref, c_ref, before_ref,
                g_ref, h_ref, sums_ref, win, v_hi, v_lo, win2, v_hi2, v_lo2):
    depth, rows, columns = res_ref.shape
    inner = rows - EDGE
    odd = odd_ref[0]
    damp = damp_ref[0]
    late_rows(border, odd, res_ref, res_far_ref, r_ref, win, v_hi, v_lo)
    late_rows(border, odd, f_ref, f_far_ref, r_ref, win2, v_hi2, v_lo2)
    sums_ref[...] = before_ref[...]
    for o in range(depth):
        g_edge, h_edge = along_columns(((v_hi, v_lo), (v_hi2, v_lo2)), c_ref, o, EDGE, columns, depth)
        for at, count, g, h in (
            (pl.multiple_of(odd * inner, EDGE), EDGE, g_edge, h_edge),
            (pl.multiple_of((1 - odd) * EDGE, EDGE), inner, g_in_ref[o], h_in_ref[o]),
        ):
            here = pl.ds(at, count)
            g = g - damp * x_ref[o, here, :]
            h = h + damp * p_ref[o, here, :]
            g_ref[o, here, :] = g
            h_ref[o, here, :] = h
            sums_ref[3:4, :] += folded(g * g)
            sums_ref[4:5, :] += folded(g * h)
            sums_ref[5:6, :] += folded(h * h)


def last_late(odd, damp, res, res_far, g_in, x, image, image_far, h_in, p, r, c, before, border):
    depth, rows, columns = res.shape
    return pl.pallas_call(
        functools.partial(last_kernel, border),
        out_shape=(f32(depth, rows, columns), f32(depth, rows, columns), f32(8, LANE)),
        in_specs=[SM, SM] + [VM] * 11,
        out_specs=[VM] * 3,
        scratch_shapes=late_scratch(depth, columns, EDGE) * 2,
        compiler_params=params(),
        cost_estimate=cost(2.6),
        name="last_late",
    )(odd, damp, res, res_far, g_in, x, image, image_far, h_in, p, r, c, before)


def final_kernel(damp_ref, mine_ref, other_ref, x_ref, r_ref, p_ref, f_ref, g_ref, h_ref,
                 nx_out, nr_out, ng_out, np_out, nx, nr, ng, nd, sems):
    depth = x_ref.shape[0]
    damp = damp_ref[0]
    sums = jnp.sum(mine_ref[...] + other_ref[...], axis=1, keepdims=True)
    before, image, direction, gg, gh, hh = (sums[k:k + 1, :] for k in range(6))
    step = before / (image + damp * direction)
    after = gg - step * (2.0 * gh - step * hh)
    ratio = after / before
    copies = []
    for o in range(depth):
        p = p_ref[o]
        new = g_ref[o] - step * h_ref[o]
        for k, (buf, out, value) in enumerate((
            (nx, nx_out, x_ref[o] + step * p),
            (nr, nr_out, r_ref[o] - step * f_ref[o]),
            (ng, ng_out, new),
            (nd, np_out, new + ratio * p),
        )):
            buf[o] = value
            copies.append(pltpu.make_async_copy(buf.at[o], out.at[o], sems.at[o, k]))
            copies[-1].start()
    for c in copies:
        c.wait()


def final(damp, mine, other, x, r, p, f, g, h):
    shape = x.shape
    return pl.pallas_call(
        final_kernel,
        out_shape=(f32(*shape),) * 4,
        in_specs=[SM] + [VM] * 8,
        out_specs=[ANY] * 4,
        scratch_shapes=[pltpu.VMEM(shape, F32)] * 4 + [pltpu.SemaphoreType.DMA((shape[0], 4))],
        compiler_params=params(),
        cost_estimate=cost(2.0),
        name="final",
    )(damp, mine, other, x, r, p, f, g, h)


def swap(values, axis, step):
    return lax.ppermute(values, axis, [(i, i ^ step) for i in range(lax.axis_size(axis))])


def body(solution, residual, gradient, direction, row_taps, col_taps, damping):
    border = row_taps.shape[2] // 2
    depth, rows, columns = direction.shape
    inner = rows - EDGE
    peers = lax.axis_size("lat")
    odd = lax.axis_index("lat") % 2
    odd_arr = jnp.full((1,), odd, jnp.int32)
    far_pairs = [p for a in range(1, peers - 1, 2) for p in ((a, a + 1), (a + 1, a))]

    def near_swap(v):
        return swap(v, "lat", 1)

    def far_swap(v):
        return lax.ppermute(v, "lat", far_pairs)

    place = lax.axis_index("lat")
    more = jnp.full((1,), jnp.where(odd == 1, place < peers - 1, place > 0), jnp.int32)

    p_far_edge, p_near_edge = edges(odd_arr, direction, odd_arr, 2 * EDGE, EDGE)
    p_far, p_near = far_swap(p_far_edge), near_swap(p_near_edge)
    re, rl, c, rae, ral, ca, sums = prep(row_taps, col_taps, inner, direction)

    r_far_edge = lax.dynamic_slice_in_dim(residual, odd * inner, EDGE, axis=1)
    r_near_edge = lax.dynamic_slice_in_dim(residual, (1 - odd) * inner, EDGE, axis=1)
    p_near, r_near_edge = lax.optimization_barrier((p_near, r_near_edge))
    r_near = near_swap(r_near_edge)
    image_in = early(odd_arr, direction, p_near, re, c, border)
    f_near = near_swap(lax.dynamic_slice_in_dim(image_in, (1 - odd) * (inner - EDGE), EDGE, axis=1))
    g_in = early(odd_arr, residual, r_near, rae, ca, border)
    g_in, r_far_edge = lax.optimization_barrier((g_in, r_far_edge))
    r_far = far_swap(r_far_edge)
    image, f_far, sums = image_late(odd_arr, more, direction, p_far, rl, c, image_in, gradient, sums, g_in, border)
    h_in = early(odd_arr, image, f_near, rae, ca, border)
    g, h, sums = last_late(odd_arr, damping, residual, r_far, g_in, solution, image, f_far, h_in, direction, ral, ca, sums, border)

    step = 1
    while 2 * step < peers:
        step *= 2
    while step > 1:
        sums = sums + swap(sums, "lat", step)
        step //= 2
    other = swap(sums, "lat", step)
    return final(damping, sums, other, solution, residual, direction, image, g, h)


def solution(mesh):
    split_rows = P("stack", "lat", None)
    return jax.shard_map(
        body,
        mesh=mesh,
        in_specs=(split_rows,) * 4 + (P(),) * 3,
        out_specs=(split_rows,) * 4,
        check_vma=False,
    )
```

```python
import functools

import jax
import jax.numpy as jnp
from jax import lax
from jax.experimental import pallas as pl
from jax.experimental.pallas import tpu as pltpu
from jax.sharding import PartitionSpec as P

F32 = jnp.float32
BF16 = jnp.bfloat16
EDGE = 16
LANE = 128
WIDE = 256
VM = pl.BlockSpec(memory_space=pltpu.VMEM)
SM = pl.BlockSpec(memory_space=pltpu.SMEM)
ANY = pl.BlockSpec(memory_space=pl.ANY)
LIMIT = 20 * 2**20


def split(x):
    hi = x.astype(BF16)
    return hi, (x - hi.astype(F32)).astype(BF16)


def params():
    return pltpu.CompilerParams(vmem_limit_bytes=LIMIT)


def cost(us):
    return pl.CostEstimate(flops=int(us * 1.0e9), bytes_accessed=1 << 20, transcendentals=0)


def f32(*shape):
    return jax.ShapeDtypeStruct(shape, F32)


def edges_kernel(odd_ref, v_ref, after_ref, far_out, near_out, sems):
    rows = v_ref.shape[1]
    odd = odd_ref[0]
    copies = []
    for k, (side, dst) in enumerate(((odd, far_out), (1 - odd, near_out))):
        count = dst.shape[1]
        here = pl.ds(pl.multiple_of(side * (rows - count), EDGE), count)
        copies.append(pltpu.make_async_copy(v_ref.at[:, here, :], dst, sems.at[k]))
    for c in copies:
        c.start()
    for c in copies:
        c.wait()


def edges(odd, v, after, far, near):
    depth, rows, columns = v.shape
    return pl.pallas_call(
        edges_kernel,
        out_shape=(f32(depth, far, columns), f32(depth, near, columns)),
        in_specs=[SM, VM, ANY],
        out_specs=[VM] * 2,
        scratch_shapes=[pltpu.SemaphoreType.DMA((2,))],
        compiler_params=params(),
        cost_estimate=cost(0.2),
        name="edges",
    )(odd, v, after)


def one_hot(count, at):
    tap = lax.broadcasted_iota(jnp.int32, (count, WIDE), 0)
    lane = lax.broadcasted_iota(jnp.int32, (count, WIDE), 1)
    return jnp.where(lane == (at(tap) + WIDE) % WIDE, 1.0, 0.0).astype(BF16)


def pick(parts_and_places):
    got = None
    for part, place in parts_and_places:
        term = jnp.dot(part, place, preferred_element_type=F32)
        got = term if got is None else got + term
    return got


def prep_kernel(depth, inner, row_ref, col_ref, p_ref, *refs):
    outs, sums_ref, bases = refs[:6], refs[6], refs[7:]
    sums_ref[...] = jnp.zeros_like(sums_ref)
    for o in range(depth):
        sums_ref[2:3, :] += folded(p_ref[o] * p_ref[o])
    count = row_ref.shape[1]
    last = count - 1
    row_hi, row_lo = split(row_ref[...])
    col_hi, col_lo = split(col_ref[...])
    window = LANE + 2 * EDGE
    lane = lax.broadcasted_iota(jnp.int32, (window, WIDE), 1)
    back = lax.broadcasted_iota(jnp.int32, (window, WIDE), 0) - jnp.where(lane < LANE, lane, lane - LANE)
    inside = (back >= 0) & (back <= last)
    for adjoint in (False, True):
        r_early, r_late, c_out = outs[3:] if adjoint else outs[:3]
        tall = EDGE if adjoint else 2 * EDGE
        turn = (lambda a: last - a) if adjoint else (lambda a: a)
        for base, gap in ((bases[0], inner + 2 * EDGE), (bases[1], tall + 2 * EDGE)):
            base[...] = pick((
                (row_hi, one_hot(count, turn)),
                (row_hi, one_hot(count, lambda a: turn(a) + gap)),
                (row_lo, one_hot(count, lambda a: turn(a) + 2 * gap)),
            ))
        bases[2][...] = pick(((col_hi, one_hot(count, lambda a: -turn(a))), (col_lo, one_hot(count, lambda a: LANE - turn(a)))))

        def banded(base, pair, rows, shift):
            wide = jnp.broadcast_to(base[pl.ds(pair, 1), :], (rows, WIDE))
            return pltpu.roll(wide, shift, 1, stride=1, stride_axis=0)

        for o in range(depth):
            for s in range(depth):
                pair = s * depth + o if adjoint else o * depth + s
                r_early[s, o * inner:(o + 1) * inner, :] = banded(bases[0], pair, inner, 1).astype(BF16)
                r_late[s, o * tall:(o + 1) * tall, :] = banded(bases[1], pair, tall, 1).astype(BF16)
                band = jnp.where(inside, banded(bases[2], pair, window, 0), 0.0)
                c_out[o, s * WIDE:s * WIDE + window, :] = band.astype(BF16)
                c_out[o, s * WIDE + window:(s + 1) * WIDE, :] = jnp.zeros((WIDE - window, WIDE), BF16)


def prep(row, col, inner, direction):
    depth, _, count = row.shape
    pairs = depth * depth

    def bands(tall):
        return (
            jax.ShapeDtypeStruct((depth, depth * inner, WIDE), BF16),
            jax.ShapeDtypeStruct((depth, depth * tall, WIDE), BF16),
            jax.ShapeDtypeStruct((depth, depth * WIDE, WIDE), BF16),
        )

    return pl.pallas_call(
        functools.partial(prep_kernel, depth, inner),
        out_shape=bands(2 * EDGE) + bands(EDGE) + (f32(8, LANE),),
        in_specs=[VM] * 3,
        out_specs=[VM] * 7,
        scratch_shapes=[pltpu.VMEM((pairs, WIDE), F32)] * 3,
        compiler_params=params(),
        cost_estimate=cost(1.5),
        name="prep",
    )(row.reshape(pairs, count), col.reshape(pairs, count), direction)


def shifted(x, border):
    wide = jnp.concatenate([x, jnp.zeros((x.shape[0], LANE), F32)], axis=1)
    return split(pltpu.roll(wide, border, 1))


def put(win, at, group, hi, lo):
    rows = hi.shape[0]
    for g, part in enumerate((hi, lo, hi)):
        win[pl.ds(pl.multiple_of(at + g * group, EDGE), rows), :] = part


def along_rows(r_ref, win, v_hi, v_lo, s, group):
    if 3 * group < WIDE:
        win[s, 3 * group:, :] = jnp.zeros((WIDE - 3 * group, win.shape[2]), BF16)
    got = jnp.dot(r_ref[s], win[s], preferred_element_type=F32)
    v_hi[s], v_lo[s] = split(got)


def along_columns(sources, c_ref, o, rows, columns, depth):
    tall = []
    blocks = columns // LANE
    for pair in sources:
        for part in pair:
            for n in range(blocks):
                tall.append(jnp.concatenate(
                    [part[s, o * rows:(o + 1) * rows, n * LANE:n * LANE + WIDE] for s in range(depth)], axis=1))
    got = jnp.dot(jnp.concatenate(tall, axis=0), c_ref[o], preferred_element_type=F32)
    planes = []
    for k in range(len(sources)):
        out = []
        for n in range(blocks):
            at = (2 * k * blocks + n) * rows
            top, low = got[at:at + rows], got[at + blocks * rows:at + (blocks + 1) * rows]
            out.append(top[:, :LANE] + (top[:, LANE:] + low[:, :LANE]))
        planes.append(jnp.concatenate(out, axis=1))
    return planes


def folded(x):
    part = jnp.sum(x.reshape(x.shape[0] // 8, 8, x.shape[1]), axis=0)
    part = sum(part[:, n:n + LANE] for n in range(0, x.shape[1], LANE))
    return jnp.sum(part, axis=0, keepdims=True)


def early_kernel(border, odd_ref, v_ref, near_ref, r_ref, c_ref, out_ref, win, v_hi, v_lo):
    depth, rows, columns = v_ref.shape
    inner = rows - EDGE
    group = rows + EDGE
    odd = odd_ref[0]
    for s in range(depth):
        put(win.at[s], odd * EDGE, group, *shifted(v_ref[s], border))
        put(win.at[s], (1 - odd) * rows, group, *shifted(near_ref[s], border))
        along_rows(r_ref, win, v_hi, v_lo, s, group)
    for o in range(depth):
        out_ref[o], = along_columns(((v_hi, v_lo),), c_ref, o, inner, columns, depth)


def early(odd, v, near, r, c, border):
    depth, rows, columns = v.shape
    inner = rows - EDGE
    wide = columns + LANE
    return pl.pallas_call(
        functools.partial(early_kernel, border),
        out_shape=f32(depth, inner, columns),
        in_specs=[SM, VM, VM, VM, VM],
        out_specs=VM,
        scratch_shapes=[
            pltpu.VMEM((depth, WIDE, wide), BF16),
            pltpu.VMEM((depth, depth * inner, wide), BF16),
            pltpu.VMEM((depth, depth * inner, wide), BF16),
        ],
        compiler_params=params(),
        cost_estimate=cost(2.8),
        name="early",
    )(odd, v, near, r, c)


def late_rows(border, odd, v_ref, far_ref, r_ref, win, v_hi, v_lo):
    depth, rows, _ = v_ref.shape
    beyond = far_ref.shape[1]
    group = beyond + 2 * EDGE
    start = pl.multiple_of(odd * (rows - 2 * EDGE), EDGE)
    for s in range(depth):
        put(win.at[s], (1 - odd) * beyond, group, *shifted(v_ref[s, pl.ds(start, 2 * EDGE), :], border))
        put(win.at[s], odd * 2 * EDGE, group, *shifted(far_ref[s], border))
        along_rows(r_ref, win, v_hi, v_lo, s, group)


def late_scratch(depth, columns, tall):
    wide = columns + LANE
    return [
        pltpu.VMEM((depth, WIDE, wide), BF16),
        pltpu.VMEM((depth, depth * tall, wide), BF16),
        pltpu.VMEM((depth, depth * tall, wide), BF16),
    ]


def image_kernel(border, odd_ref, more_ref, v_ref, far_ref, r_ref, c_ref, in_ref, grad_ref, before_ref, after_ref, out_ref, beyond_ref, sums_ref, win, v_hi, v_lo):
    depth, rows, columns = v_ref.shape
    inner = rows - EDGE
    odd = odd_ref[0]
    more = more_ref[0]
    late_rows(border, odd, v_ref, far_ref, r_ref, win, v_hi, v_lo)
    sums_ref[...] = before_ref[...]
    for o in range(depth):
        both, = along_columns(((v_hi, v_lo),), c_ref, o, 2 * EDGE, columns, depth)
        first, second = both[:EDGE], both[EDGE:]
        edge = jnp.where(odd == 1, first, second)
        beyond_ref[o] = jnp.where(more == 1, jnp.where(odd == 1, second, first), 0.0)
        out_ref[o, pl.ds(pl.multiple_of(odd * inner, EDGE), EDGE), :] = edge
        out_ref[o, pl.ds(pl.multiple_of((1 - odd) * EDGE, EDGE), inner), :] = in_ref[o]
        sums_ref[0:1, :] += folded(grad_ref[o] * grad_ref[o])
        sums_ref[1:2, :] += folded(in_ref[o] * in_ref[o]) + folded(edge * edge)


def image_late(odd, more, v, far, r, c, inside, grad, before, after, border):
    depth, rows, columns = v.shape
    return pl.pallas_call(
        functools.partial(image_kernel, border),
        out_shape=(f32(depth, rows, columns), f32(depth, EDGE, columns), f32(8, LANE)),
        in_specs=[SM, SM] + [VM] * 7 + [ANY],
        out_specs=[VM] * 3,
        scratch_shapes=late_scratch(depth, columns, 2 * EDGE),
        compiler_params=params(),
        cost_estimate=cost(2.0),
        name="image_late",
    )(odd, more, v, far, r, c, inside, grad, before, after)


def last_kernel(border, odd_ref, damp_ref, res_ref, res_far_ref, g_in_ref, x_ref, f_ref, f_far_ref, h_in_ref, p_ref, r_ref, c_ref, before_ref,
                g_ref, h_ref, sums_ref, win, v_hi, v_lo, win2, v_hi2, v_lo2):
    depth, rows, columns = res_ref.shape
    inner = rows - EDGE
    odd = odd_ref[0]
    damp = damp_ref[0]
    late_rows(border, odd, res_ref, res_far_ref, r_ref, win, v_hi, v_lo)
    late_rows(border, odd, f_ref, f_far_ref, r_ref, win2, v_hi2, v_lo2)
    sums_ref[...] = before_ref[...]
    for o in range(depth):
        g_edge, h_edge = along_columns(((v_hi, v_lo), (v_hi2, v_lo2)), c_ref, o, EDGE, columns, depth)
        for at, count, g, h in (
            (pl.multiple_of(odd * inner, EDGE), EDGE, g_edge, h_edge),
            (pl.multiple_of((1 - odd) * EDGE, EDGE), inner, g_in_ref[o], h_in_ref[o]),
        ):
            here = pl.ds(at, count)
            g = g - damp * x_ref[o, here, :]
            h = h + damp * p_ref[o, here, :]
            g_ref[o, here, :] = g
            h_ref[o, here, :] = h
            sums_ref[3:4, :] += folded(g * g)
            sums_ref[4:5, :] += folded(g * h)
            sums_ref[5:6, :] += folded(h * h)


def last_late(odd, damp, res, res_far, g_in, x, image, image_far, h_in, p, r, c, before, border):
    depth, rows, columns = res.shape
    return pl.pallas_call(
        functools.partial(last_kernel, border),
        out_shape=(f32(depth, rows, columns), f32(depth, rows, columns), f32(8, LANE)),
        in_specs=[SM, SM] + [VM] * 11,
        out_specs=[VM] * 3,
        scratch_shapes=late_scratch(depth, columns, EDGE) * 2,
        compiler_params=params(),
        cost_estimate=cost(2.6),
        name="last_late",
    )(odd, damp, res, res_far, g_in, x, image, image_far, h_in, p, r, c, before)


def final_kernel(damp_ref, mine_ref, other_ref, x_ref, r_ref, p_ref, f_ref, g_ref, h_ref,
                 nx_out, nr_out, ng_out, np_out, nx, nr, ng, nd, sems):
    depth = x_ref.shape[0]
    damp = damp_ref[0]
    sums = jnp.sum(mine_ref[...] + other_ref[...], axis=1, keepdims=True)
    before, image, direction, gg, gh, hh = (sums[k:k + 1, :] for k in range(6))
    step = before / (image + damp * direction)
    after = gg - step * (2.0 * gh - step * hh)
    ratio = after / before
    copies = []
    for o in range(depth):
        p = p_ref[o]
        new = g_ref[o] - step * h_ref[o]
        for k, (buf, out, value) in enumerate((
            (nx, nx_out, x_ref[o] + step * p),
            (nr, nr_out, r_ref[o] - step * f_ref[o]),
            (ng, ng_out, new),
            (nd, np_out, new + ratio * p),
        )):
            buf[o] = value
            copies.append(pltpu.make_async_copy(buf.at[o], out.at[o], sems.at[o, k]))
            copies[-1].start()
    for c in copies:
        c.wait()


def final(damp, mine, other, x, r, p, f, g, h):
    shape = x.shape
    return pl.pallas_call(
        final_kernel,
        out_shape=(f32(*shape),) * 4,
        in_specs=[SM] + [VM] * 8,
        out_specs=[ANY] * 4,
        scratch_shapes=[pltpu.VMEM(shape, F32)] * 4 + [pltpu.SemaphoreType.DMA((shape[0], 4))],
        compiler_params=params(),
        cost_estimate=cost(2.0),
        name="final",
    )(damp, mine, other, x, r, p, f, g, h)


def swap(values, axis, step):
    return lax.ppermute(values, axis, [(i, i ^ step) for i in range(lax.axis_size(axis))])


def body(solution, residual, gradient, direction, row_taps, col_taps, damping):
    border = row_taps.shape[2] // 2
    depth, rows, columns = direction.shape
    inner = rows - EDGE
    peers = lax.axis_size("lat")
    odd = lax.axis_index("lat") % 2
    odd_arr = jnp.full((1,), odd, jnp.int32)
    far_pairs = [p for a in range(1, peers - 1, 2) for p in ((a, a + 1), (a + 1, a))]

    def near_swap(v):
        return swap(v, "lat", 1)

    def far_swap(v):
        return lax.ppermute(v, "lat", far_pairs)

    place = lax.axis_index("lat")
    more = jnp.full((1,), jnp.where(odd == 1, place < peers - 1, place > 0), jnp.int32)

    p_far_edge, p_near_edge = edges(odd_arr, direction, odd_arr, 2 * EDGE, EDGE)
    p_far, p_near = far_swap(p_far_edge), near_swap(p_near_edge)
    re, rl, c, rae, ral, ca, sums = prep(row_taps, col_taps, inner, direction)

    r_far_edge = lax.dynamic_slice_in_dim(residual, odd * inner, EDGE, axis=1)
    r_near_edge = lax.dynamic_slice_in_dim(residual, (1 - odd) * inner, EDGE, axis=1)
    p_near, r_near_edge = lax.optimization_barrier((p_near, r_near_edge))
    r_near = near_swap(r_near_edge)
    image_in = early(odd_arr, direction, p_near, re, c, border)
    f_near = near_swap(lax.dynamic_slice_in_dim(image_in, (1 - odd) * (inner - EDGE), EDGE, axis=1))
    g_in = early(odd_arr, residual, r_near, rae, ca, border)
    g_in, r_far_edge = lax.optimization_barrier((g_in, r_far_edge))
    r_far = far_swap(r_far_edge)
    image, f_far, sums = image_late(odd_arr, more, direction, p_far, rl, c, image_in, gradient, sums, g_in, border)
    h_in = early(odd_arr, image, f_near, rae, ca, border)
    g, h, sums = last_late(odd_arr, damping, residual, r_far, g_in, solution, image, f_far, h_in, direction, ral, ca, sums, border)

    step = 1
    while 2 * step < peers:
        step *= 2
    rounds = [step >> k for k in range(step.bit_length())]
    rounds[:2] = rounds[1::-1]
    for step in rounds[:-1]:
        sums = sums + swap(sums, "lat", step)
    other = swap(sums, "lat", rounds[-1])
    return final(damping, sums, other, solution, residual, direction, image, g, h)


def solution(mesh):
    split_rows = P("stack", "lat", None)
    return jax.shard_map(
        body,
        mesh=mesh,
        in_specs=(split_rows,) * 4 + (P(),) * 3,
        out_specs=(split_rows,) * 4,
        check_vma=False,
    )
```
